512 devices in a mesh: tm: 16 (over x, z_hi, core), cell: 32 (over y, z_lo).
Axes of the slice: x: 4, y: 8, z: 8 (z_hi: 2, z_lo: 4; z = z_hi * 4 + z_lo), core: 2. Of those that a mesh axis runs over, the one named last changes fastest.
Arguments:
- sensitivity: bfloat16 [2048, 16, 16384], P(None, 'tm', 'cell'), may hold values from -0.25 to 0.25
- duals: bfloat16 [2048, 128], P(('tm', 'cell')), may hold values from -6 to 6
- time_cov: float32 [16, 16], replicated, may hold values from 0.05 to 0.5
- cell_coords: int32 [2, 16384], P(None, 'cell'), may hold values from 0 to 127, as said below
- obs_time: int32 [2048], replicated, may hold values from 0 to 15
- obs_owner: int32 [2048], replicated, may hold values from 0 to 2047, each once
Outputs:
- product: float32 [2048, 128], P(('tm', 'cell'))
The draws below stay inside these ranges and needn't reach their ends.
Inputs may be any that keep to these rules, and one draw needn't show every extreme that they name: `cell_coords`: every cell has its own grid position; rows lie below 128 and columns below 128. `obs_owner`: every observation stands in exactly one slot.
All inputs are finite; a program needn't handle non-finite values.
Results may differ from the reference program's by a relative error of at most 0.0049.
Values may be sent and summed in bfloat16 or wider, within the bound.
No kernel may reach another device: no remote copies, remote signals or barrier semaphores. Data moves between devices by JAX's collectives and lax.ppermute only.
A program may use at most 64 MiB of HBM per device.

```python
import jax
import jax.numpy as jnp
from jax import lax

OBS = 2048
REALS = 128
GRID_COLS = 128
LSCALE = 4
TIMES = 16
CELLS = 16384


def draw_cell_coords(key, part):
    placed = jax.random.permutation(jax.random.fold_in(key, 17), CELLS).astype(jnp.int32)
    return jnp.stack([placed // GRID_COLS, placed % GRID_COLS]).astype(jnp.int32)


def plant(drawn, stream_key, low, largest):
    longest = drawn.shape.index(max(drawn.shape))
    spots = []
    for shift in (0, 1):
        where = [jax.random.randint(jax.random.fold_in(stream_key, axis), (), 0, length) for axis, length in enumerate(drawn.shape)]
        where[longest] = (where[longest] + shift) % drawn.shape[longest]
        spots.append(tuple(where))
    return drawn.at[spots[0]].set(low).at[spots[1]].set(largest)


def raised(array, stream_key, source, target, blocks, factor):
    owner, partner = [(jnp.arange(array.shape[axis_at]) // (array.shape[axis_at] // blocks)).reshape([-1 if axis == axis_at else 1 for axis in range(array.ndim)]) for axis_at in (source, target)]
    chosen = jax.random.permutation(stream_key, blocks)[partner]
    strong = (owner == chosen) | (owner == (partner + blocks // 2) % blocks)
    return jnp.where(strong, factor * array, array)


def levels(own_key, shape, cuts, least, high):
    def one(dim, parts):
        draws = jax.random.uniform(jax.random.fold_in(jax.random.fold_in(own_key, 6), dim), (parts,), jnp.float32, least / len(cuts), high / len(cuts))
        return jnp.repeat(jnp.exp(draws), shape[dim] // parts).reshape((-1,) + (1,) * (len(shape) - dim - 1))

    gain = one(*cuts[0])
    for cut in cuts[1:]:
        gain = gain * one(*cut)
    return gain


def normal_values(stream_key, shape, deviation, limit, cuts=(), kind=jnp.bfloat16):
    drawn = jax.random.normal(stream_key, shape, jnp.float32) * deviation
    if len(cuts) > 0:
        drawn = levels(stream_key, shape, cuts, -0.22, 0.18) * drawn
    return jnp.clip(drawn, min=-limit, max=limit).astype(kind)


def gaussian_with(key, dims, scale, reach, shards, heavy, kind=jnp.bfloat16):
    array = scale * jax.random.normal(key, dims, jnp.float32)
    if shards:
        array = array * levels(key, dims, shards, -0.22, 0.18)
    return jnp.clip(raised(array, jax.random.fold_in(key, 3), *heavy), -reach, reach).astype(kind)


def setup_inputs(seed: int = 0) -> dict:
    splits = jax.random.split(jax.random.key(seed), 7)
    return {
        "sensitivity": gaussian_with(splits[0], (OBS, TIMES, CELLS), OBS ** -0.5, 0.25, ((1, 16), (2, 32)), (2, 0, 32, 2.75)),
        "duals": normal_values(splits[1], (OBS, REALS), 1.0, 6.0, ((0, 512),)),
        "time_cov": jnp.clip(jax.random.uniform(splits[2], (TIMES, TIMES), jnp.float32, 0.05, 0.5), 0.05, 0.5),
        "cell_coords": draw_cell_coords(jax.random.fold_in(splits[6], 71), 0),
        "obs_time": plant(jax.random.randint(splits[4], (OBS,), 0, TIMES), jax.random.fold_in(splits[4], 1), 0, TIMES - 1).astype(jnp.int32),
        "obs_owner": jax.random.permutation(splits[5], OBS).astype(jnp.int32),
    }


def covariance(left_coords, right_coords):
    row_gap = (left_coords[0][:, None] - right_coords[0][None, :]).astype(jnp.float32)
    col_gap = (left_coords[1][:, None] - right_coords[1][None, :]).astype(jnp.float32)
    distance = jnp.sqrt(row_gap * row_gap + col_gap * col_gap)
    return (jnp.exp(-distance / LSCALE) / (8.0 * LSCALE)).astype(jnp.bfloat16)

def reference(sensitivity, duals, time_cov, cell_coords, obs_time, obs_owner):
    time_index = jnp.arange(TIMES, dtype=jnp.int32)
    live = time_index[None, :, None] <= obs_time[:, None, None]
    masked = jnp.where(live, sensitivity, jnp.zeros((), jnp.bfloat16))
    flattened = masked.reshape(OBS, TIMES * CELLS)
    adjoint = jnp.dot(flattened.T, duals, preferred_element_type=jnp.float32).astype(jnp.bfloat16)
    adjoint_f = adjoint.reshape(TIMES, CELLS, REALS).astype(jnp.float32)
    mixed = jnp.einsum('st,tcr->scr', time_cov, adjoint_f, precision=lax.Precision.HIGHEST).astype(jnp.bfloat16)
    columns = mixed.transpose(1, 0, 2).reshape(CELLS, TIMES * REALS)
    width = min(512, CELLS)
    starts = jnp.arange(0, CELLS, width, dtype=jnp.int32)

    def row_block(offset):
        left_coords = lax.dynamic_slice_in_dim(cell_coords, offset, width, 1)
        kernel = covariance(left_coords, cell_coords)
        return jnp.dot(kernel, columns, preferred_element_type=jnp.float32).astype(jnp.bfloat16)
    weighted = lax.map(row_block, starts).reshape(CELLS, TIMES, REALS)
    weighted_flat = weighted.transpose(1, 0, 2).reshape(TIMES * CELLS, REALS)
    forward = jnp.dot(flattened, weighted_flat, preferred_element_type=jnp.float32)
    return forward[obs_owner]
```

```python
import functools

import jax
import jax.numpy as jnp
import ml_dtypes
import numpy as np
from jax import lax
from jax.experimental import pallas as pl
from jax.experimental.pallas import tpu as pltpu
from jax.sharding import Mesh
from jax.sharding import PartitionSpec as P

LSCALE = 4
GRID = 128
X, ZH, CO, Y, ZL = "tm_0", "tm_1", "tm_2", "cell_0", "cell_1"
CELL = (Y, ZL)
EVERY = (X, ZH, CO, Y, ZL)
BF16 = jnp.bfloat16
F32 = jnp.float32
EXACT = lax.Precision.HIGHEST


def spectrum():
    size = 2 * GRID
    gap = np.arange(GRID, dtype=np.float32)
    distance = np.sqrt(gap[:, None] * gap[:, None] + gap[None, :] * gap[None, :])
    table = (np.exp(-distance / np.float32(LSCALE)) / np.float32(8.0 * LSCALE)).astype(ml_dtypes.bfloat16)
    table = table.astype(np.float64)
    wave = np.concatenate([np.arange(GRID + 1), np.arange(1, GRID)])
    angle = 2.0 * np.pi * wave[:, None] * np.arange(GRID)[None, :] / size
    basis = np.where(np.arange(size)[:, None] <= GRID, np.cos(angle), np.sin(angle))
    edge = (wave == 0) | (wave == GRID)
    basis = basis * np.where(edge, np.sqrt(1.0 / size), np.sqrt(2.0 / size))[:, None]
    fold = np.cos(angle) * np.where(np.arange(GRID) == 0, 1.0, 2.0)[None, :]
    eigen = fold @ table @ fold.T
    return basis.astype(np.float32), eigen.astype(np.float32)


def spatial_kernel(group, weight_ref, field_ref, rows_ref, cols_ref, basis_ref, turned_ref, eigen_ref, out_ref,
                   mixed, on_row, on_col, grid):
    kept = weight_ref.shape[0]
    times = field_ref.shape[0]
    chunks = rows_ref.shape[0]
    for s in range(kept):
        total = jnp.zeros((chunks, GRID), F32)
        for t in range(times):
            total = total + weight_ref[s, t] * field_ref[t].astype(F32)
        mixed[s] = total.astype(BF16).astype(F32)
    place = lax.broadcasted_iota(jnp.int32, (GRID, GRID), 0)
    grid[...] = jnp.zeros_like(grid)

    def put(j, carry):
        first = pl.multiple_of(j * group, group)
        rows = rows_ref[pl.ds(first, group), :]
        cols = cols_ref[pl.ds(first, group), :]
        values = [mixed[s, pl.ds(first, group), :] for s in range(kept)]
        lefts = []
        rights = []
        for g in range(group):
            span = pl.ds(pl.multiple_of(first * GRID + g * GRID, GRID), GRID)
            row_hit = jnp.where(place == rows[g : g + 1, :], 1.0, 0.0).astype(BF16)
            col_hit = jnp.where(place == cols[g : g + 1, :], 1.0, 0.0).astype(BF16)
            on_row[:, span] = row_hit
            on_col[:, span] = col_hit
            lefts.append(
                jnp.concatenate([row_hit * values[s][g : g + 1, :].astype(BF16) for s in range(kept)], axis=0)
            )
            rights.append(col_hit)
        grid[...] += lax.dot_general(
            jnp.concatenate(lefts, axis=1),
            jnp.concatenate(rights, axis=1),
            (((1,), (1,)), ((), ())),
            preferred_element_type=F32,
        )
        return carry

    lax.fori_loop(0, chunks // group, put, 0)
    basis = basis_ref[...]
    turned = turned_ref[...]
    ahead = jnp.dot(grid[...], turned, precision=EXACT, preferred_element_type=F32)
    for s in range(kept):
        span = slice(s * GRID, (s + 1) * GRID)
        waves = jnp.dot(basis, ahead[span], precision=EXACT, preferred_element_type=F32) * eigen_ref[...]
        back = jnp.dot(turned, waves, precision=EXACT, preferred_element_type=F32)
        grid[span, :] = jnp.dot(back, basis, precision=EXACT, preferred_element_type=F32)
    smooth = grid[...].astype(BF16)

    def take(j, carry):
        first = pl.multiple_of(j * group, group)
        span = pl.ds(pl.multiple_of(first * GRID, group * GRID), group * GRID)
        picked = jnp.dot(smooth, on_col[:, span], preferred_element_type=F32)
        row_hit = on_row[:, span].astype(F32)
        for s in range(kept):
            line = jnp.sum(picked[s * GRID : (s + 1) * GRID] * row_hit, axis=0, keepdims=True)
            block = jnp.concatenate([line[:, g * GRID : (g + 1) * GRID] for g in range(group)], axis=0)
            out_ref[pl.ds(pl.multiple_of(s * chunks + first, group), group), :] = block.astype(BF16)
        return carry

    lax.fori_loop(0, chunks // group, take, 0)


def spatial(weight, field, rows, cols):
    kept = weight.shape[0]
    chunks = field.shape[1]
    cells = chunks * GRID
    basis, eigen = spectrum()
    vmem = pl.BlockSpec(memory_space=pltpu.VMEM)
    return pl.pallas_call(
        functools.partial(spatial_kernel, 16),
        out_shape=jax.ShapeDtypeStruct((kept * chunks, GRID), BF16),
        in_specs=[pl.BlockSpec(memory_space=pltpu.SMEM)] + [vmem] * 6,
        out_specs=vmem,
        scratch_shapes=[
            pltpu.VMEM((kept, chunks, GRID), F32),
            pltpu.VMEM((GRID, cells), BF16),
            pltpu.VMEM((GRID, cells), BF16),
            pltpu.VMEM((kept * GRID, GRID), F32),
        ],
        compiler_params=pltpu.CompilerParams(vmem_limit_bytes=40 << 20),
    )(weight, field, rows, cols, jnp.asarray(basis), jnp.asarray(basis.T.copy()), jnp.asarray(eigen))


def exchange(pieces, axes):
    return lax.all_to_all(pieces, axes, split_axis=0, concat_axis=0, tiled=True)


def copies(array, axes):
    return exchange(jnp.broadcast_to(array, (lax.axis_size(axes), *array.shape)), axes)


def per_device(sensitivity, duals, time_cov, cell_coords, obs_time, obs_owner):
    obs = sensitivity.shape[0]
    reals = duals.shape[1]
    flat = sensitivity.reshape(obs, -1)
    here = lax.axis_index((X, ZH, CO))
    live = here <= obs_time
    quarter = lax.axis_size(X)
    kept = time_cov.shape[0] // quarter
    weight = lax.dynamic_slice_in_dim(time_cov, lax.axis_index(X) * kept, kept, 0)

    own = duals.shape[0]
    places = cell_coords.astype(BF16).reshape(-1, GRID)
    half = places.shape[0] // 2
    first = copies(jnp.concatenate([duals, places], axis=0), CELL)
    rows = first[:, own : own + half].reshape(-1, GRID).astype(jnp.int32)
    cols = first[:, own + half :].reshape(-1, GRID).astype(jnp.int32)
    second = copies(first[:, :own].reshape(-1, reals), (X, ZH))
    third = lax.all_gather(second, CO, axis=0)
    all_duals = third.transpose(1, 0, 2, 3).reshape(obs, reals)

    seen = jnp.where(live[:, None], all_duals, jnp.zeros((), BF16))
    adjoint = lax.dot_general(seen, flat, (((0,), (0,)), ((), ())), preferred_element_type=F32).astype(BF16)
    pieces = jnp.broadcast_to(adjoint.reshape(1, reals, -1, GRID), (quarter, reals, flat.shape[1] // GRID, GRID))
    field = exchange(pieces.reshape(-1, *pieces.shape[2:]), EVERY)
    field = field.reshape(time_cov.shape[0], -1, GRID)

    weighted = spatial(weight, field, rows, cols)
    weighted = exchange(weighted.reshape(reals, -1, GRID), (ZH, CO, Y, ZL)).reshape(reals, -1)

    forward = lax.dot_general(flat, weighted, (((1,), (1,)), ((), ())), preferred_element_type=F32).astype(BF16)
    pair = lax.axis_size(CO)
    groups = lax.axis_size((X, ZH))
    slots = obs_owner.reshape(groups, pair, -1).transpose(1, 0, 2).reshape(-1)
    chosen = (slots[:, None] == jnp.arange(obs, dtype=jnp.int32)[None, :]) & live[None, :]
    product = jnp.dot(chosen.astype(BF16), forward, preferred_element_type=F32).astype(BF16)
    product = exchange(product.reshape(pair, -1, reals), CO)
    product = jnp.sum(product.astype(F32), axis=0).astype(BF16)
    product = exchange(product.reshape(-1, own, reals), (X, ZH, Y, ZL))
    return jnp.sum(product.astype(F32), axis=0)


def solution(mesh):
    split = Mesh(mesh.devices.reshape(4, 2, 2, 8, 4), EVERY)
    every = P(EVERY, None)
    return jax.shard_map(
        per_device,
        mesh=split,
        in_specs=(P(None, (X, ZH, CO), CELL), every, P(), P(None, CELL), P(), P()),
        out_specs=every,
        check_vma=False,
    )
```

```python
import functools

import jax
import jax.numpy as jnp
import ml_dtypes
import numpy as np
from jax import lax
from jax.experimental import pallas as pl
from jax.experimental.pallas import tpu as pltpu
from jax.sharding import Mesh
from jax.sharding import PartitionSpec as P

LSCALE = 4
GRID = 128
PARTS = 2
LOW = GRID // PARTS
X, ZH, CO, Y, ZL = "tm_0", "tm_1", "tm_2", "cell_0", "cell_1"
CELL = (Y, ZL)
EVERY = (X, ZH, CO, Y, ZL)
BF16 = jnp.bfloat16
F32 = jnp.float32
VMEM = pl.BlockSpec(memory_space=pltpu.VMEM)
SMEM = pl.BlockSpec(memory_space=pltpu.SMEM)


def halves(array):
    high = array.astype(np.float32).astype(ml_dtypes.bfloat16)
    return high, (array - high.astype(np.float64)).astype(np.float32).astype(ml_dtypes.bfloat16)


def spectrum():
    size = 2 * GRID
    gap = np.arange(GRID, dtype=np.float32)
    distance = np.sqrt(gap[:, None] * gap[:, None] + gap[None, :] * gap[None, :])
    table = (np.exp(-distance / np.float32(LSCALE)) / np.float32(8.0 * LSCALE)).astype(ml_dtypes.bfloat16)
    table = table.astype(np.float64)
    wave = np.concatenate([np.arange(GRID + 1), np.arange(1, GRID)])
    angle = 2.0 * np.pi * wave[:, None] * np.arange(GRID)[None, :] / size
    basis = np.where(np.arange(size)[:, None] <= GRID, np.cos(angle), np.sin(angle))
    edge = (wave == 0) | (wave == GRID)
    basis = basis * np.where(edge, np.sqrt(1.0 / size), np.sqrt(2.0 / size))[:, None]
    fold = np.cos(angle) * np.where(np.arange(GRID) == 0, 1.0, 2.0)[None, :]
    eigen = fold @ table @ fold.T
    return (*halves(basis), *halves(basis.T), eigen.astype(np.float32))


def matmul(a, b):
    return jnp.dot(a, b, preferred_element_type=F32)


def parted(a):
    high = a.astype(BF16)
    return high, (a - high.astype(F32)).astype(BF16)


def matmul_parted(a, b):
    return matmul(a[0], b[0]) + (matmul(a[0], b[1]) + matmul(a[1], b[0]))


def places_kernel(rows_ref, cols_ref, low_ref, wide_ref, turned_ref):
    wide_at = lax.broadcasted_iota(jnp.int32, (PARTS * GRID, GRID), 0)
    low_at = lax.broadcasted_iota(jnp.int32, (LOW, GRID), 0)
    rows = rows_ref[...]
    low = rows % LOW
    wide = (rows // LOW) * GRID + cols_ref[...]
    for g in range(rows.shape[0]):
        span = slice(g * GRID, (g + 1) * GRID)
        low_ref[:, span] = jnp.where(low_at == low[g : g + 1, :], 1.0, 0.0).astype(BF16)
        hit = jnp.where(wide_at == wide[g : g + 1, :], 1.0, 0.0).astype(BF16)
        wide_ref[:, span] = hit
        turned_ref[span, :] = hit.T


def places(rows, cols):
    cells = rows.size
    wide = PARTS * GRID
    lot = 8
    return pl.pallas_call(
        places_kernel,
        grid=(rows.shape[0] // lot,),
        out_shape=[
            jax.ShapeDtypeStruct((LOW, cells), BF16),
            jax.ShapeDtypeStruct((wide, cells), BF16),
            jax.ShapeDtypeStruct((cells, wide), BF16),
        ],
        in_specs=[pl.BlockSpec((lot, GRID), lambda i: (i, 0))] * 2,
        out_specs=[
            pl.BlockSpec((LOW, lot * GRID), lambda i: (0, i)),
            pl.BlockSpec((wide, lot * GRID), lambda i: (0, i)),
            pl.BlockSpec((lot * GRID, wide), lambda i: (i, 0)),
        ],
        compiler_params=pltpu.CompilerParams(vmem_limit_bytes=56 << 20),
        cost_estimate=pl.CostEstimate(flops=10**9, bytes_accessed=18 << 20, transcendentals=0),
    )(rows, cols)


def spatial_kernel(lot, lot_back, kept, which_ref, weight_ref, field_ref, low_hbm, wide_hbm, turned_hbm,
                   basis_h, basis_l, side_h, side_l, eigen_ref, out_ref, mixed, grid,
                   low_ref, wide_ref, turned_ref, low_done, wide_done, turned_done):
    times, chunks, _ = field_ref.shape
    pair = 2
    which = which_ref[0]
    strides = times // kept
    lots = chunks // lot

    def turned_copy(j):
        span = pl.ds(pl.multiple_of(j * lot * GRID, lot * GRID), lot * GRID)
        return pltpu.make_async_copy(turned_hbm.at[span], turned_ref.at[span], turned_done.at[j])

    low_copy = pltpu.make_async_copy(low_hbm, low_ref, low_done)
    wide_copy = pltpu.make_async_copy(wide_hbm, wide_ref, wide_done)
    low_copy.start()
    for j in range(lots):
        turned_copy(j).start()
    wide_copy.start()

    def mix(j, carry):
        rows = pl.ds(pl.multiple_of(j * 16, 16), 16)
        totals = [None] * kept
        for k in range(times):
            t = (k % (times // pair)) * pair + k // (times // pair)
            value = field_ref[k, rows, :].astype(F32)
            for s in range(kept):
                term = weight_ref[s * strides + which, t] * value
                totals[s] = term if k == 0 else totals[s] + term
        for s in range(kept):
            mixed[s, rows, :] = totals[s].astype(BF16).astype(F32)
        return carry

    lax.fori_loop(0, chunks // 16, mix, 0)
    grid[...] = jnp.zeros_like(grid)
    low_copy.wait()

    def put(j, carry):
        turned_copy(j).wait()
        first = pl.multiple_of(j * lot, lot)
        values = [mixed[s, pl.ds(first, lot), :] for s in range(kept)]
        lefts = []
        for g in range(lot):
            hit = low_ref[:, pl.ds(pl.multiple_of((first + g) * GRID, GRID), GRID)]
            lines = [jnp.broadcast_to(v[g : g + 1, :], (16, GRID)).astype(BF16) for v in values]
            lefts.append(
                jnp.concatenate([hit[k : k + 16] * line for line in lines for k in range(0, LOW, 16)], axis=0)
            )
        span = pl.ds(pl.multiple_of(first * GRID, lot * GRID), lot * GRID)
        grid[...] += matmul(jnp.concatenate(lefts, axis=1), turned_ref[span, :])
        return carry

    lax.fori_loop(0, lots, put, 0)
    basis = (basis_h[...], basis_l[...])
    side = (side_h[...], side_l[...])
    whole = jnp.concatenate(
        [
            grid[s * LOW : (s + 1) * LOW, p * GRID : (p + 1) * GRID]
            for s in range(kept)
            for p in range(PARTS)
        ],
        axis=0,
    )
    ahead = matmul_parted(parted(whole), side)
    for s in range(kept):
        waves = matmul_parted(basis, parted(ahead[s * GRID : (s + 1) * GRID])) * eigen_ref[...]
        back = matmul_parted(side, parted(waves))
        smooth = matmul_parted(parted(back), basis)
        for p in range(PARTS):
            grid[s * LOW : (s + 1) * LOW, p * GRID : (p + 1) * GRID] = smooth[p * LOW : (p + 1) * LOW]
    weighted = grid[...].astype(BF16)
    wide_copy.wait()

    def take(j, carry):
        first = pl.multiple_of(j * lot_back, lot_back)
        span = pl.ds(pl.multiple_of(first * GRID, lot_back * GRID), lot_back * GRID)
        picked = matmul(weighted, wide_ref[:, span])
        hit = low_ref[:, span].astype(F32)
        for s in range(kept):
            line = jnp.sum(picked[s * LOW : (s + 1) * LOW] * hit, axis=0, keepdims=True)
            block = jnp.concatenate([line[:, g * GRID : (g + 1) * GRID] for g in range(lot_back)], axis=0)
            out_ref[pl.ds(pl.multiple_of(s * chunks + first, lot_back), lot_back), :] = block.astype(BF16)
        return carry

    lax.fori_loop(0, chunks // lot_back, take, 0)


def spatial(which, weight, field, spots, kept):
    chunks = field.shape[1]
    constants = [jnp.asarray(c) for c in spectrum()]
    lot = 16
    return pl.pallas_call(
        functools.partial(spatial_kernel, lot, 32, kept),
        out_shape=jax.ShapeDtypeStruct((kept * chunks, GRID), BF16),
        in_specs=[SMEM] * 2 + [VMEM] + [pl.BlockSpec(memory_space=pl.ANY)] * len(spots) + [VMEM] * len(constants),
        out_specs=VMEM,
        scratch_shapes=[
            pltpu.VMEM((kept, chunks, GRID), F32),
            pltpu.VMEM((kept * LOW, PARTS * GRID), F32),
            *[pltpu.VMEM(spot.shape, spot.dtype) for spot in spots],
            pltpu.SemaphoreType.DMA,
            pltpu.SemaphoreType.DMA,
            pltpu.SemaphoreType.DMA((chunks // lot,)),
        ],
        compiler_params=pltpu.CompilerParams(vmem_limit_bytes=52 << 20),
        cost_estimate=pl.CostEstimate(flops=10**10, bytes_accessed=18 << 20, transcendentals=0),
    )(which, weight, field, *spots, *constants)


def exchange(pieces, axes):
    return lax.all_to_all(pieces, axes, split_axis=0, concat_axis=0, tiled=True)


def copies(array, axes):
    return exchange(jnp.broadcast_to(array, (lax.axis_size(axes), *array.shape)), axes)


def per_device(sensitivity, duals, time_cov, cell_coords, obs_time, obs_owner):
    obs = sensitivity.shape[0]
    own, reals = duals.shape
    flat = sensitivity.reshape(obs, -1)
    live = lax.axis_index((X, ZH, CO)) <= obs_time
    nx, nh, pair = (lax.axis_size(a) for a in (X, ZH, CO))
    which = lax.axis_index((ZH, CO)).reshape(1)

    line = lax.dynamic_slice_in_dim(cell_coords, lax.axis_index(ZH), 1, 0).astype(BF16).reshape(-1, GRID)
    first = copies(jnp.concatenate([duals, line], axis=0), (ZH, Y, ZL))
    coords = first[:, own:].reshape(nh, -1, GRID).astype(jnp.int32)
    second = copies(first[:, :own].reshape(-1, reals), X)
    third = lax.all_gather(second.reshape(nx * nh, -1, reals), CO, axis=0)
    all_duals = third.transpose(1, 0, 2, 3).reshape(obs, reals)

    seen = jnp.where(live[:, None], all_duals, jnp.zeros((), BF16))
    adjoint = lax.dot_general(seen, flat, (((0,), (0,)), ((), ())), preferred_element_type=F32).astype(BF16)
    pieces = adjoint.reshape(nx, 1, reals // nx, -1, GRID)
    pieces = jnp.broadcast_to(pieces, (nx, nh, *pieces.shape[2:]))
    field = exchange(pieces.reshape(-1, *pieces.shape[3:]), (X, ZH, Y, ZL))
    field = lax.all_gather(field.reshape(nx * nh, -1, GRID), CO, axis=0, tiled=True)

    spots = places(coords[0], coords[1])
    weighted = spatial(which, time_cov, field, spots, nx)
    slots, weighted = lax.optimization_barrier((obs_owner, weighted))
    weighted = exchange(weighted.reshape(reals, -1, GRID), (X, Y, ZL)).reshape(reals, -1)
    slots = slots.reshape(nx * nh, pair, -1).transpose(1, 0, 2).reshape(-1)
    chosen = (slots[:, None] == jnp.arange(obs, dtype=jnp.int32)[None, :]) & live[None, :]
    picked = jnp.dot(chosen.astype(BF16), flat, preferred_element_type=F32).astype(BF16)
    picked, weighted = lax.optimization_barrier((picked, weighted))
    product = lax.dot_general(picked, weighted, (((1,), (1,)), ((), ())), preferred_element_type=F32).astype(BF16)
    product = exchange(product.reshape(pair, -1, reals), CO)
    product = jnp.sum(product.astype(F32), axis=0).astype(BF16)
    product = exchange(product.reshape(-1, own, reals), (X, ZH, Y, ZL))
    return jnp.sum(product.astype(F32), axis=0)


def solution(mesh):
    split = Mesh(mesh.devices.reshape(4, 2, 2, 8, 4), EVERY)
    every = P(EVERY, None)
    return jax.shard_map(
        per_device,
        mesh=split,
        in_specs=(P(None, (X, ZH, CO), CELL), every, P(), P(None, CELL), P(), P()),
        out_specs=every,
        check_vma=False,
    )
```

```python
import functools

import jax
import jax.numpy as jnp
import ml_dtypes
import numpy as np
from jax import lax
from jax.experimental import pallas as pl
from jax.experimental.pallas import tpu as pltpu
from jax.sharding import Mesh
from jax.sharding import PartitionSpec as P

LSCALE = 4
GRID = 128
PARTS = 2
LOW = GRID // PARTS
X, ZH, CO, Y, ZL = "tm_0", "tm_1", "tm_2", "cell_0", "cell_1"
CELL = (Y, ZL)
EVERY = (X, ZH, CO, Y, ZL)
BF16 = jnp.bfloat16
F32 = jnp.float32
VMEM = pl.BlockSpec(memory_space=pltpu.VMEM)
SMEM = pl.BlockSpec(memory_space=pltpu.SMEM)


def halves(array):
    high = array.astype(np.float32).astype(ml_dtypes.bfloat16)
    return high, (array - high.astype(np.float64)).astype(np.float32).astype(ml_dtypes.bfloat16)


def spectrum():
    size = 2 * GRID
    gap = np.arange(GRID, dtype=np.float32)
    distance = np.sqrt(gap[:, None] * gap[:, None] + gap[None, :] * gap[None, :])
    table = (np.exp(-distance / np.float32(LSCALE)) / np.float32(8.0 * LSCALE)).astype(ml_dtypes.bfloat16)
    table = table.astype(np.float64)
    wave = np.concatenate([np.arange(GRID + 1), np.arange(1, GRID)])
    angle = 2.0 * np.pi * wave[:, None] * np.arange(GRID)[None, :] / size
    basis = np.where(np.arange(size)[:, None] <= GRID, np.cos(angle), np.sin(angle))
    edge = (wave == 0) | (wave == GRID)
    basis = basis * np.where(edge, np.sqrt(1.0 / size), np.sqrt(2.0 / size))[:, None]
    fold = np.cos(angle) * np.where(np.arange(GRID) == 0, 1.0, 2.0)[None, :]
    eigen = fold @ table @ fold.T
    return (*halves(basis), *halves(basis.T), eigen.astype(np.float32))


def matmul(a, b):
    return jnp.dot(a, b, preferred_element_type=F32)


def parted(a):
    high = a.astype(BF16)
    return high, (a - high.astype(F32)).astype(BF16)


def matmul_parted(a, b):
    return matmul(a[0], b[0]) + (matmul(a[0], b[1]) + matmul(a[1], b[0]))


def hits(at, line):
    spread = jnp.broadcast_to(line.astype(F32), (16, line.shape[1])).astype(BF16)
    one = jnp.ones(spread.shape, BF16)
    zero = jnp.zeros(spread.shape, BF16)
    return [jnp.where(rows == spread, one, zero) for rows in at]


def spatial_kernel(lot, kept, which_ref, weight_ref, field_ref, rows_ref, cols_ref,
                   basis_h, basis_l, side_h, side_l, eigen_ref, out_ref, mixed, grid, low_ref, wide_ref):
    times, chunks, _ = field_ref.shape
    pair = 2
    which = which_ref[0]
    strides = times // kept

    def mix(j, carry):
        rows = pl.ds(pl.multiple_of(j * 16, 16), 16)
        totals = [None] * kept
        for k in range(times):
            t = (k % (times // pair)) * pair + k // (times // pair)
            value = field_ref[k, rows, :].astype(F32)
            for s in range(kept):
                term = weight_ref[s * strides + which, t] * value
                totals[s] = term if k == 0 else totals[s] + term
        for s in range(kept):
            mixed[s, rows, :] = totals[s].astype(BF16).astype(F32)
        return carry

    lax.fori_loop(0, chunks // 16, mix, 0)
    grid[...] = jnp.zeros_like(grid)
    first_at = lax.broadcasted_iota(jnp.int32, (16, GRID), 0).astype(F32)
    wide_at = [(first_at + float(k)).astype(BF16) for k in range(0, PARTS * GRID, 16)]
    low_at = wide_at[: LOW // 16]

    def put(j, carry):
        first = pl.multiple_of(j * lot, lot)
        values = [mixed[s, pl.ds(first, lot), :] for s in range(kept)]
        rows = rows_ref[pl.ds(first, lot), :]
        low = rows % LOW
        wide = (rows // LOW) * GRID + cols_ref[pl.ds(first, lot), :]
        lefts = []
        rights = []
        for g in range(lot):
            span = pl.ds(pl.multiple_of((first + g) * GRID, GRID), GRID)
            low_hit = hits(low_at, low[g : g + 1, :])
            wide_hit = jnp.concatenate(hits(wide_at, wide[g : g + 1, :]), axis=0)
            lines = [jnp.broadcast_to(v[g : g + 1, :], (16, GRID)).astype(BF16) for v in values]
            lefts.append(jnp.concatenate([hit * line for line in lines for hit in low_hit], axis=0))
            rights.append(wide_hit)
            low_ref[:, span] = jnp.concatenate(low_hit, axis=0)
            wide_ref[:, span] = wide_hit
        grid[...] += lax.dot_general(
            jnp.concatenate(lefts, axis=1),
            jnp.concatenate(rights, axis=1),
            (((1,), (1,)), ((), ())),
            preferred_element_type=F32,
        )
        return carry

    lax.fori_loop(0, chunks // lot, put, 0)
    basis = (basis_h[...], basis_l[...])
    side = (side_h[...], side_l[...])
    whole = jnp.concatenate(
        [
            grid[s * LOW : (s + 1) * LOW, p * GRID : (p + 1) * GRID]
            for s in range(kept)
            for p in range(PARTS)
        ],
        axis=0,
    )
    ahead = matmul_parted(parted(whole), side)
    for s in range(kept):
        waves = matmul_parted(basis, parted(ahead[s * GRID : (s + 1) * GRID])) * eigen_ref[...]
        back = matmul_parted(side, parted(waves))
        smooth = matmul_parted(parted(back), basis)
        for p in range(PARTS):
            grid[s * LOW : (s + 1) * LOW, p * GRID : (p + 1) * GRID] = smooth[p * LOW : (p + 1) * LOW]
    weighted = grid[...].astype(BF16)

    def take(j, carry):
        first = pl.multiple_of(j * lot, lot)
        span = pl.ds(pl.multiple_of(first * GRID, lot * GRID), lot * GRID)
        picked = matmul(weighted, wide_ref[:, span])
        hit = low_ref[:, span].astype(F32)
        for s in range(kept):
            line = jnp.sum(picked[s * LOW : (s + 1) * LOW] * hit, axis=0, keepdims=True)
            block = jnp.concatenate([line[:, g * GRID : (g + 1) * GRID] for g in range(lot)], axis=0)
            out_ref[pl.ds(pl.multiple_of(s * chunks + first, lot), lot), :] = block.astype(BF16)
        return carry

    lax.fori_loop(0, chunks // lot, take, 0)


def spatial(which, weight, field, rows, cols, kept):
    chunks = field.shape[1]
    constants = [jnp.asarray(c) for c in spectrum()]
    return pl.pallas_call(
        functools.partial(spatial_kernel, 64, kept),
        out_shape=jax.ShapeDtypeStruct((kept * chunks, GRID), BF16),
        in_specs=[SMEM] * 2 + [VMEM] * (3 + len(constants)),
        out_specs=VMEM,
        scratch_shapes=[
            pltpu.VMEM((kept, chunks, GRID), F32),
            pltpu.VMEM((kept * LOW, PARTS * GRID), F32),
            pltpu.VMEM((LOW, chunks * GRID), BF16),
            pltpu.VMEM((PARTS * GRID, chunks * GRID), BF16),
        ],
        compiler_params=pltpu.CompilerParams(vmem_limit_bytes=48 << 20),
        cost_estimate=pl.CostEstimate(flops=10**10, bytes_accessed=18 << 20, transcendentals=0),
    )(which, weight, field, rows, cols, *constants)


def opening_kernel(half_ref, duals_ref, coords_ref, out_ref):
    width = coords_ref.shape[1]
    picked = jnp.where(half_ref[0] == 0, coords_ref[0:1, :], coords_ref[1:2, :]).astype(F32)
    lines = [picked[:, k : k + GRID] for k in range(0, width, GRID)]
    block = jnp.concatenate([duals_ref[...].astype(F32), *lines], axis=0).astype(BF16)
    out_ref[...] = jnp.broadcast_to(block, out_ref.shape)


def opening(half, duals, coords, count):
    rows = duals.shape[0] + coords.shape[1] // GRID
    return pl.pallas_call(
        opening_kernel,
        out_shape=jax.ShapeDtypeStruct((count, rows, GRID), BF16),
        in_specs=[SMEM, VMEM, VMEM],
        out_specs=VMEM,
    )(half, duals, coords)


def exchange(pieces, axes):
    return lax.all_to_all(pieces, axes, split_axis=0, concat_axis=0, tiled=True)


def copies(array, axes):
    return exchange(jnp.broadcast_to(array, (lax.axis_size(axes), *array.shape)), axes)


def per_device(sensitivity, duals, time_cov, cell_coords, obs_time, obs_owner):
    obs = sensitivity.shape[0]
    own, reals = duals.shape
    flat = sensitivity.reshape(obs, -1)
    live = lax.axis_index((X, ZH, CO)) <= obs_time
    nx, nh, pair = (lax.axis_size(a) for a in (X, ZH, CO))
    which = lax.axis_index((ZH, CO)).reshape(1)

    plane = (ZH, Y, ZL)
    first = exchange(opening(lax.axis_index(ZH).reshape(1), duals, cell_coords, lax.axis_size(plane)), plane)
    coords = first[:, own:].reshape(nh, -1, GRID).astype(jnp.int32)
    second = copies(first[:, :own].reshape(-1, reals), X)
    third = lax.all_gather(second.reshape(nx * nh, -1, reals), CO, axis=0)
    all_duals = third.transpose(1, 0, 2, 3).reshape(obs, reals)

    seen = jnp.where(live[:, None], all_duals, jnp.zeros((), BF16))
    adjoint = lax.dot_general(seen, flat, (((0,), (0,)), ((), ())), preferred_element_type=F32).astype(BF16)
    pieces = adjoint.reshape(nx, 1, reals // nx, -1, GRID)
    pieces = jnp.broadcast_to(pieces, (nx, nh, *pieces.shape[2:]))
    pieces, slots = lax.optimization_barrier((pieces, obs_owner))
    field = exchange(pieces.reshape(-1, *pieces.shape[3:]), (X, ZH, Y, ZL))
    slots = slots.reshape(nx * nh, pair, -1).transpose(1, 0, 2).reshape(-1)
    chosen = (slots[:, None] == jnp.arange(obs, dtype=jnp.int32)[None, :]) & live[None, :]
    picked = jnp.dot(chosen.astype(BF16), flat, preferred_element_type=F32).astype(BF16)
    field, picked = lax.optimization_barrier((field, picked))
    field = lax.all_gather(field.reshape(nx * nh, -1, GRID), CO, axis=0, tiled=True)

    weighted = spatial(which, time_cov, field, coords[0], coords[1], nx)
    weighted = exchange(weighted.reshape(reals, -1, GRID), (X, Y, ZL)).reshape(reals, -1)
    product = lax.dot_general(picked, weighted, (((1,), (1,)), ((), ())), preferred_element_type=F32).astype(BF16)
    product = exchange(product.reshape(pair, -1, reals), CO)
    product = jnp.sum(product.astype(F32), axis=0).astype(BF16)
    product = exchange(product.reshape(-1, own, reals), (X, ZH, Y, ZL))
    return jnp.sum(product.astype(F32), axis=0)


def solution(mesh):
    split = Mesh(mesh.devices.reshape(4, 2, 2, 8, 4), EVERY)
    every = P(EVERY, None)
    return jax.shard_map(
        per_device,
        mesh=split,
        in_specs=(P(None, (X, ZH, CO), CELL), every, P(), P(None, CELL), P(), P()),
        out_specs=every,
        check_vma=False,
    )
```

```python
import functools

import jax
import jax.numpy as jnp
import ml_dtypes
import numpy as np
from jax import lax
from jax.experimental import pallas as pl
from jax.experimental.pallas import tpu as pltpu
from jax.sharding import Mesh
from jax.sharding import PartitionSpec as P

LSCALE = 4
GRID = 128
PARTS = 2
LOW = GRID // PARTS
X, ZH, CO, Y, ZL = "tm_0", "tm_1", "tm_2", "cell_0", "cell_1"
CELL = (Y, ZL)
EVERY = (X, ZH, CO, Y, ZL)
BF16 = jnp.bfloat16
F32 = jnp.float32
VMEM = pl.BlockSpec(memory_space=pltpu.VMEM)
SMEM = pl.BlockSpec(memory_space=pltpu.SMEM)


def halves(array):
    high = array.astype(np.float32).astype(ml_dtypes.bfloat16)
    return high, (array - high.astype(np.float64)).astype(np.float32).astype(ml_dtypes.bfloat16)


def spectrum():
    size = 2 * GRID
    gap = np.arange(GRID, dtype=np.float32)
    distance = np.sqrt(gap[:, None] * gap[:, None] + gap[None, :] * gap[None, :])
    table = (np.exp(-distance / np.float32(LSCALE)) / np.float32(8.0 * LSCALE)).astype(ml_dtypes.bfloat16)
    table = table.astype(np.float64)
    wave = np.concatenate([np.arange(GRID + 1), np.arange(1, GRID)])
    angle = 2.0 * np.pi * wave[:, None] * np.arange(GRID)[None, :] / size
    basis = np.where(np.arange(size)[:, None] <= GRID, np.cos(angle), np.sin(angle))
    edge = (wave == 0) | (wave == GRID)
    basis = basis * np.where(edge, np.sqrt(1.0 / size), np.sqrt(2.0 / size))[:, None]
    fold = np.cos(angle) * np.where(np.arange(GRID) == 0, 1.0, 2.0)[None, :]
    eigen = fold @ table @ fold.T
    return (*halves(basis), *halves(basis.T), eigen.astype(np.float32))


def matmul(a, b):
    return jnp.dot(a, b, preferred_element_type=F32)


def parted(a):
    high = a.astype(BF16)
    return high, (a - high.astype(F32)).astype(BF16)


def matmul_parted(a, b):
    return matmul(a[0], b[0]) + (matmul(a[0], b[1]) + matmul(a[1], b[0]))


def hits(at, line):
    spread = jnp.broadcast_to(line.astype(F32), (16, line.shape[1])).astype(BF16)
    one = jnp.ones(spread.shape, BF16)
    zero = jnp.zeros(spread.shape, BF16)
    return [jnp.where(rows == spread, one, zero) for rows in at]


def spatial_kernel(lot, kept, folds, which_ref, cov_ref, field_ref, rows_ref, cols_ref,
                   basis_h, basis_l, side_h, side_l, eigen_ref, out_ref, mixed, grid, low_ref, wide_ref):
    chunks = rows_ref.shape[0]
    sets = field_ref.shape[0]
    height = kept * folds
    blocks = chunks // folds
    times = cov_ref.shape[1]
    pair = 2
    high = sets // pair
    which = which_ref[0]
    line = lax.broadcasted_iota(jnp.int32, (height, times * folds), 0)
    column = lax.broadcasted_iota(jnp.int32, (height, times * folds), 1)
    weight = jnp.zeros(line.shape, F32)
    for k in range(times):
        core, rest = divmod(k, times // pair)
        half, place = divmod(rest, times // sets)
        t = (place * high + half) * pair + core
        for s in range(kept):
            here = (line // folds == s) & (column // folds == k)
            weight = jnp.where(here, cov_ref[s * sets + which, t], weight)
    weight = jnp.where(line % folds == column % folds, weight, 0.0)
    first_part = weight.astype(BF16)
    rest = weight - first_part.astype(F32)
    second_part = rest.astype(BF16)
    third_part = (rest - second_part.astype(F32)).astype(BF16)
    parts = jnp.concatenate([first_part, second_part, third_part], axis=0)
    tall = field_ref.shape[1] // blocks
    for c in range(0, blocks, 8):
        columns = [
            jnp.concatenate([field_ref[k, (c + i) * tall : (c + i + 1) * tall, :] for k in range(sets)], axis=0)
            for i in range(8)
        ]
        got = matmul(parts, jnp.concatenate(columns, axis=1))
        total = got[2 * height :] + got[height : 2 * height] + got[:height]
        mixed[:, c * GRID : (c + 8) * GRID] = total.astype(BF16).astype(F32)
    grid[...] = jnp.zeros_like(grid)
    first_at = lax.broadcasted_iota(jnp.int32, (16, GRID), 0).astype(F32)
    wide_at = [(first_at + float(k)).astype(BF16) for k in range(0, PARTS * GRID, 16)]
    low_at = wide_at[: LOW // 16]

    def put(j, carry):
        first = pl.multiple_of(j * lot, lot)
        length = lot // folds * GRID
        values = mixed[:, pl.ds(pl.multiple_of(j * length, length), length)]
        rows = rows_ref[pl.ds(first, lot), :]
        low = rows % LOW
        wide = (rows // LOW) * GRID + cols_ref[pl.ds(first, lot), :]
        lefts = []
        rights = []
        for g in range(lot):
            span = pl.ds(pl.multiple_of((first + g) * GRID, GRID), GRID)
            low_hit = hits(low_at, low[g : g + 1, :])
            wide_hit = jnp.concatenate(hits(wide_at, wide[g : g + 1, :]), axis=0)
            column = slice(g // folds * GRID, (g // folds + 1) * GRID)
            tops = [s * folds + g % folds for s in range(kept)]
            lines = [jnp.broadcast_to(values[k : k + 1, column], (16, GRID)).astype(BF16) for k in tops]
            lefts.append(jnp.concatenate([hit * line for line in lines for hit in low_hit], axis=0))
            rights.append(wide_hit)
            low_ref[:, span] = jnp.concatenate(low_hit, axis=0)
            wide_ref[:, span] = wide_hit
        grid[...] += lax.dot_general(
            jnp.concatenate(lefts, axis=1),
            jnp.concatenate(rights, axis=1),
            (((1,), (1,)), ((), ())),
            preferred_element_type=F32,
        )
        return carry

    lax.fori_loop(0, chunks // lot, put, 0)
    basis = (basis_h[...], basis_l[...])
    side = (side_h[...], side_l[...])
    whole = jnp.concatenate(
        [
            grid[s * LOW : (s + 1) * LOW, p * GRID : (p + 1) * GRID]
            for s in range(kept)
            for p in range(PARTS)
        ],
        axis=0,
    )
    exact = whole.astype(BF16)
    ahead = matmul(exact, side[0]) + matmul(exact, side[1])
    for s in range(kept):
        waves = matmul_parted(basis, parted(ahead[s * GRID : (s + 1) * GRID])) * eigen_ref[...]
        back = matmul_parted(side, parted(waves))
        smooth = matmul_parted(parted(back), basis)
        for p in range(PARTS):
            grid[s * LOW : (s + 1) * LOW, p * GRID : (p + 1) * GRID] = smooth[p * LOW : (p + 1) * LOW]
    weighted = grid[...].astype(BF16)

    def take(j, carry):
        first = pl.multiple_of(j * lot, lot)
        span = pl.ds(pl.multiple_of(first * GRID, lot * GRID), lot * GRID)
        picked = matmul(weighted, wide_ref[:, span])
        hit = low_ref[:, span].astype(F32)
        for s in range(kept):
            line = jnp.sum(picked[s * LOW : (s + 1) * LOW] * hit, axis=0, keepdims=True)
            block = jnp.concatenate([line[:, g * GRID : (g + 1) * GRID] for g in range(lot)], axis=0)
            out_ref[pl.ds(pl.multiple_of(s * chunks + first, lot), lot), :] = block.astype(BF16)
        return carry

    lax.fori_loop(0, chunks // lot, take, 0)


def spatial(which, time_cov, field, rows, cols, kept, folds):
    chunks = rows.shape[0]
    constants = [jnp.asarray(c) for c in spectrum()]
    return pl.pallas_call(
        functools.partial(spatial_kernel, 64, kept, folds),
        out_shape=jax.ShapeDtypeStruct((kept * chunks, GRID), BF16),
        in_specs=[SMEM] * 2 + [VMEM] * (3 + len(constants)),
        out_specs=VMEM,
        scratch_shapes=[
            pltpu.VMEM((kept * folds, chunks // folds * GRID), F32),
            pltpu.VMEM((kept * LOW, PARTS * GRID), F32),
            pltpu.VMEM((LOW, chunks * GRID), BF16),
            pltpu.VMEM((PARTS * GRID, chunks * GRID), BF16),
        ],
        compiler_params=pltpu.CompilerParams(vmem_limit_bytes=48 << 20),
        cost_estimate=pl.CostEstimate(flops=10**10, bytes_accessed=18 << 20, transcendentals=0),
    )(which, time_cov, field, rows, cols, *constants)


def opening_kernel(half_ref, duals_ref, coords_ref, out_ref):
    width = coords_ref.shape[1]
    picked = jnp.where(half_ref[0] == 0, coords_ref[0:1, :], coords_ref[1:2, :]).astype(F32)
    lines = [picked[:, k : k + GRID] for k in range(0, width, GRID)]
    block = jnp.concatenate([duals_ref[...].astype(F32), *lines], axis=0).astype(BF16)
    out_ref[...] = jnp.broadcast_to(block, out_ref.shape)


def opening(half, duals, coords, count):
    rows = duals.shape[0] + coords.shape[1] // GRID
    return pl.pallas_call(
        opening_kernel,
        out_shape=jax.ShapeDtypeStruct((count, rows, GRID), BF16),
        in_specs=[SMEM, VMEM, VMEM],
        out_specs=VMEM,
    )(half, duals, coords)


def exchange(pieces, axes):
    return lax.all_to_all(pieces, axes, split_axis=0, concat_axis=0, tiled=True)


def copies(array, axes):
    return exchange(jnp.broadcast_to(array, (lax.axis_size(axes), *array.shape)), axes)


def per_device(sensitivity, duals, time_cov, cell_coords, obs_time, obs_owner):
    obs = sensitivity.shape[0]
    own, reals = duals.shape
    flat = sensitivity.reshape(obs, -1)
    live = lax.axis_index((X, ZH, CO)) <= obs_time
    nx, nh, pair = (lax.axis_size(a) for a in (X, ZH, CO))
    which = lax.axis_index((ZH, CO)).reshape(1)

    plane = (ZH, Y, ZL)
    first = exchange(opening(lax.axis_index(ZH).reshape(1), duals, cell_coords, lax.axis_size(plane)), plane)
    coords = first[:, own:].reshape(nh, -1, GRID).astype(jnp.int32)
    second = copies(first[:, :own].reshape(-1, reals), X)
    third = lax.all_gather(second.reshape(nx * nh, -1, reals), CO, axis=0)
    all_duals = third.transpose(1, 0, 2, 3).reshape(obs, reals)

    seen = jnp.where(live[:, None], all_duals, jnp.zeros((), BF16))
    adjoint = lax.dot_general(seen, flat, (((0,), (0,)), ((), ())), preferred_element_type=F32).astype(BF16)
    folds = flat.shape[1] // GRID
    part = reals // nx
    pieces = exchange(adjoint.reshape(nx, part, folds, GRID), X)
    slots = obs_owner.reshape(nx * nh, pair, -1).transpose(1, 0, 2).reshape(-1)
    pieces, slots = lax.optimization_barrier((pieces, slots))
    pieces = jnp.broadcast_to(pieces.transpose(1, 0, 2, 3)[None], (nh, part, nx, folds, GRID))
    field = exchange(pieces.reshape(-1, nx * folds, GRID), plane)

    chosen = (slots[:, None] == jnp.arange(obs, dtype=jnp.int32)[None, :]) & live[None, :]
    picked = jnp.dot(chosen.astype(BF16), flat, preferred_element_type=F32).astype(BF16)
    field, picked = lax.optimization_barrier((field, picked))
    field = lax.all_gather(field.reshape(nh, -1, GRID), CO, axis=0, tiled=True)

    weighted = spatial(which, time_cov, field, coords[0], coords[1], nx, folds)
    weighted = exchange(weighted.reshape(reals, -1, GRID), (X, Y, ZL)).reshape(reals, -1)
    product = lax.dot_general(picked, weighted, (((1,), (1,)), ((), ())), preferred_element_type=F32).astype(BF16)
    product = exchange(product.reshape(pair, -1, reals), CO)
    product = jnp.sum(product.astype(F32), axis=0).astype(BF16)
    product = exchange(product.reshape(nx, -1, reals), X)
    product = jnp.sum(product.astype(F32), axis=0).astype(BF16)
    product = exchange(product.reshape(-1, own, reals), plane)
    return jnp.sum(product.astype(F32), axis=0)


def solution(mesh):
    split = Mesh(mesh.devices.reshape(4, 2, 2, 8, 4), EVERY)
    every = P(EVERY, None)
    return jax.shard_map(
        per_device,
        mesh=split,
        in_specs=(P(None, (X, ZH, CO), CELL), every, P(), P(None, CELL), P(), P()),
        out_specs=every,
        check_vma=False,
    )
```

```python
import functools

import jax
import jax.numpy as jnp
import ml_dtypes
import numpy as np
from jax import lax
from jax.experimental import pallas as pl
from jax.experimental.pallas import tpu as pltpu
from jax.sharding import Mesh
from jax.sharding import PartitionSpec as P

LSCALE = 4
GRID = 128
PARTS = 2
LOW = GRID // PARTS
X, ZH, CO, Y, ZL = "tm_0", "tm_1", "tm_2", "cell_0", "cell_1"
CELL = (Y, ZL)
EVERY = (X, ZH, CO, Y, ZL)
BF16 = jnp.bfloat16
F32 = jnp.float32
VMEM = pl.BlockSpec(memory_space=pltpu.VMEM)
SMEM = pl.BlockSpec(memory_space=pltpu.SMEM)


def halves(array):
    high = array.astype(np.float32).astype(ml_dtypes.bfloat16)
    return high, (array - high.astype(np.float64)).astype(np.float32).astype(ml_dtypes.bfloat16)


def spectrum():
    size = 2 * GRID
    gap = np.arange(GRID, dtype=np.float32)
    distance = np.sqrt(gap[:, None] * gap[:, None] + gap[None, :] * gap[None, :])
    table = (np.exp(-distance / np.float32(LSCALE)) / np.float32(8.0 * LSCALE)).astype(ml_dtypes.bfloat16)
    table = table.astype(np.float64)
    wave = np.concatenate([np.arange(GRID + 1), np.arange(1, GRID)])
    angle = 2.0 * np.pi * wave[:, None] * np.arange(GRID)[None, :] / size
    basis = np.where(np.arange(size)[:, None] <= GRID, np.cos(angle), np.sin(angle))
    edge = (wave == 0) | (wave == GRID)
    basis = basis * np.where(edge, np.sqrt(1.0 / size), np.sqrt(2.0 / size))[:, None]
    fold = np.cos(angle) * np.where(np.arange(GRID) == 0, 1.0, 2.0)[None, :]
    eigen = fold @ table @ fold.T
    return (*halves(basis), *halves(basis.T), eigen.astype(np.float32))


def matmul(a, b):
    return jnp.dot(a, b, preferred_element_type=F32)


def parted(a):
    high = a.astype(BF16)
    return high, (a - high.astype(F32)).astype(BF16)


def matmul_parted(a, b):
    return matmul(a[0], b[0]) + (matmul(a[0], b[1]) + matmul(a[1], b[0]))


def hits(at, line):
    spread = jnp.broadcast_to(line.astype(F32), (16, line.shape[1])).astype(BF16)
    one = jnp.ones(spread.shape, BF16)
    zero = jnp.zeros(spread.shape, BF16)
    return [jnp.where(rows == spread, one, zero) for rows in at]


def spatial_kernel(lot, kept, which_ref, weight_ref, field_ref, rows_ref, cols_ref,
                   basis_h, basis_l, side_h, side_l, eigen_ref, out_ref, mixed, grid):
    times, chunks, _ = field_ref.shape
    pair = 2
    which = which_ref[0]
    strides = times // kept

    def mix(j, carry):
        rows = pl.ds(pl.multiple_of(j * 16, 16), 16)
        totals = [None] * kept
        for k in range(times):
            t = (k % (times // pair)) * pair + k // (times // pair)
            value = field_ref[k, rows, :].astype(F32)
            for s in range(kept):
                term = weight_ref[s * strides + which, t] * value
                totals[s] = term if k == 0 else totals[s] + term
        for s in range(kept):
            mixed[s, rows, :] = totals[s].astype(BF16).astype(F32)
        return carry

    lax.fori_loop(0, chunks // 16, mix, 0)
    grid[...] = jnp.zeros_like(grid)
    first_at = lax.broadcasted_iota(jnp.int32, (16, GRID), 0).astype(F32)
    wide_at = [(first_at + float(k)).astype(BF16) for k in range(0, PARTS * GRID, 16)]
    low_at = wide_at[: LOW // 16]

    def put(j, carry):
        first = pl.multiple_of(j * lot, lot)
        values = [mixed[s, pl.ds(first, lot), :] for s in range(kept)]
        rows = rows_ref[pl.ds(first, lot), :]
        low = rows % LOW
        wide = (rows // LOW) * GRID + cols_ref[pl.ds(first, lot), :]
        lefts = []
        rights = []
        for g in range(lot):
            low_hit = hits(low_at, low[g : g + 1, :])
            lines = [jnp.broadcast_to(v[g : g + 1, :], (16, GRID)).astype(BF16) for v in values]
            lefts.append(jnp.concatenate([hit * line for line in lines for hit in low_hit], axis=0))
            rights.append(jnp.concatenate(hits(wide_at, wide[g : g + 1, :]), axis=0))
        grid[...] += lax.dot_general(
            jnp.concatenate(lefts, axis=1),
            jnp.concatenate(rights, axis=1),
            (((1,), (1,)), ((), ())),
            preferred_element_type=F32,
        )
        return carry

    lax.fori_loop(0, chunks // lot, put, 0)
    basis = (basis_h[...], basis_l[...])
    side = (side_h[...], side_l[...])
    whole = jnp.concatenate(
        [
            grid[s * LOW : (s + 1) * LOW, p * GRID : (p + 1) * GRID]
            for s in range(kept)
            for p in range(PARTS)
        ],
        axis=0,
    )
    exact = whole.astype(BF16)
    ahead = matmul(exact, side[0]) + matmul(exact, side[1])
    for s in range(kept):
        waves = matmul_parted(basis, parted(ahead[s * GRID : (s + 1) * GRID])) * eigen_ref[...]
        back = matmul_parted(side, parted(waves))
        smooth = matmul_parted(parted(back), basis)
        for p in range(PARTS):
            grid[s * LOW : (s + 1) * LOW, p * GRID : (p + 1) * GRID] = smooth[p * LOW : (p + 1) * LOW]
    weighted = grid[...].astype(BF16)

    line_at = lax.broadcasted_iota(jnp.int32, (LOW, GRID), 0)

    def take(j, carry):
        first = pl.multiple_of(j * lot, lot)
        rows = rows_ref[pl.ds(first, lot), :]
        low = rows % LOW
        wide = (rows // LOW) * GRID + cols_ref[pl.ds(first, lot), :]
        rights = [jnp.concatenate(hits(wide_at, wide[g : g + 1, :]), axis=0) for g in range(lot)]
        picked = matmul(weighted, jnp.concatenate(rights, axis=1))
        hit = [line_at == low[g : g + 1, :] for g in range(lot)]
        for s in range(kept):
            lines = []
            for g in range(lot):
                block = picked[s * LOW : (s + 1) * LOW, g * GRID : (g + 1) * GRID]
                lines.append(jnp.sum(jnp.where(hit[g], block, 0.0), axis=0, keepdims=True))
            span = pl.ds(pl.multiple_of(s * chunks + first, lot), lot)
            out_ref[span, :] = jnp.concatenate(lines, axis=0).astype(BF16)
        return carry

    lax.fori_loop(0, chunks // lot, take, 0)


def spatial(which, weight, field, rows, cols, kept):
    chunks = field.shape[1]
    constants = [jnp.asarray(c) for c in spectrum()]
    return pl.pallas_call(
        functools.partial(spatial_kernel, 64, kept),
        out_shape=jax.ShapeDtypeStruct((kept * chunks, GRID), BF16),
        in_specs=[SMEM] * 2 + [VMEM] * (3 + len(constants)),
        out_specs=VMEM,
        scratch_shapes=[
            pltpu.VMEM((kept, chunks, GRID), F32),
            pltpu.VMEM((kept * LOW, PARTS * GRID), F32),
        ],
        compiler_params=pltpu.CompilerParams(vmem_limit_bytes=48 << 20),
        cost_estimate=pl.CostEstimate(flops=10**10, bytes_accessed=18 << 20, transcendentals=0),
    )(which, weight, field, rows, cols, *constants)


def opening_kernel(half_ref, duals_ref, coords_ref, out_ref):
    width = coords_ref.shape[1]
    picked = jnp.where(half_ref[0] == 0, coords_ref[0:1, :], coords_ref[1:2, :]).astype(F32)
    lines = [picked[:, k : k + GRID] for k in range(0, width, GRID)]
    block = jnp.concatenate([duals_ref[...].astype(F32), *lines], axis=0).astype(BF16)
    out_ref[...] = jnp.broadcast_to(block, out_ref.shape)


def opening(half, duals, coords, count):
    rows = duals.shape[0] + coords.shape[1] // GRID
    return pl.pallas_call(
        opening_kernel,
        out_shape=jax.ShapeDtypeStruct((count, rows, GRID), BF16),
        in_specs=[SMEM, VMEM, VMEM],
        out_specs=VMEM,
    )(half, duals, coords)


def adjoint_kernel(here_ref, time_ref, duals_ref, flat_ref, out_ref):
    pair, groups, rows, reals = duals_ref.shape
    outer, again, part, folds, _ = out_ref.shape
    times = time_ref[...].astype(F32).T
    here = here_ref[0].astype(F32)
    seen = []
    for k in range(pair * groups):
        block = duals_ref[k % pair, k // pair].astype(F32)
        seen.append(jnp.where(times[:, k : k + 1] >= here, block, 0.0).astype(BF16))
    total = lax.dot_general(
        jnp.concatenate(seen, axis=0), flat_ref[...], (((0,), (0,)), ((), ())), preferred_element_type=F32
    )
    pieces = jnp.stack([total[:, k * GRID : (k + 1) * GRID] for k in range(folds)], axis=1).astype(BF16)
    for i in range(outer):
        for j in range(again):
            out_ref[i, j] = pieces[i * part : (i + 1) * part]


def adjoint(here, obs_time, duals, flat, outer, again):
    rows, reals = duals.shape[2:]
    return pl.pallas_call(
        adjoint_kernel,
        out_shape=jax.ShapeDtypeStruct((outer, again, reals // outer, flat.shape[1] // GRID, GRID), BF16),
        in_specs=[SMEM] + [VMEM] * 3,
        out_specs=VMEM,
        compiler_params=pltpu.CompilerParams(vmem_limit_bytes=24 << 20),
    )(here, obs_time.reshape(-1, rows), duals, flat)


def exchange(pieces, axes):
    return lax.all_to_all(pieces, axes, split_axis=0, concat_axis=0, tiled=True)


def copies(array, axes):
    return exchange(jnp.broadcast_to(array, (lax.axis_size(axes), *array.shape)), axes)


def per_device(sensitivity, duals, time_cov, cell_coords, obs_time, obs_owner):
    obs = sensitivity.shape[0]
    own, reals = duals.shape
    flat = sensitivity.reshape(obs, -1)
    here = lax.axis_index((X, ZH, CO))
    nx, nh, pair = (lax.axis_size(a) for a in (X, ZH, CO))
    which = lax.axis_index((ZH, CO)).reshape(1)

    plane = (ZH, Y, ZL)
    first = exchange(opening(lax.axis_index(ZH).reshape(1), duals, cell_coords, lax.axis_size(plane)), plane)
    coords = first[:, own:].reshape(nh, -1, GRID).astype(jnp.int32)
    second = copies(first[:, :own].reshape(-1, reals), X)
    third = lax.all_gather(second.reshape(nx * nh, -1, reals), CO, axis=0)
    pieces = adjoint(here.reshape(1), obs_time, third, flat, nx, nh)
    core = lax.axis_index(CO)
    slots = obs_owner.reshape(nx * nh, pair, -1)
    slots = jnp.concatenate([lax.dynamic_index_in_dim(slots, i, 1, keepdims=False) for i in (1 - core, core)])
    live = here <= obs_time
    pieces, slots, live = lax.optimization_barrier((pieces, slots, live))
    field = exchange(pieces.reshape(-1, *pieces.shape[3:]), (X, ZH, Y, ZL))
    chosen = (slots.reshape(-1)[:, None] == jnp.arange(obs, dtype=jnp.int32)[None, :]) & live[None, :]
    picked = jnp.dot(chosen.astype(BF16), flat, preferred_element_type=F32).astype(BF16)
    field, picked = lax.optimization_barrier((field, picked))
    field = lax.all_gather(field.reshape(nx * nh, -1, GRID), CO, axis=0, tiled=True)

    weighted = spatial(which, time_cov, field, coords[0], coords[1], nx)
    weighted = exchange(weighted.reshape(reals, -1, GRID), (X, Y, ZL)).reshape(reals, -1)
    theirs, ours = (
        lax.dot_general(rows, weighted, (((1,), (1,)), ((), ())), preferred_element_type=F32)
        for rows in jnp.split(picked, pair)
    )
    swapped = lax.all_gather(theirs.astype(BF16), CO, axis=0)
    got = lax.dynamic_index_in_dim(swapped, 1 - core, 0, keepdims=False)
    product = (ours + got.astype(F32)).astype(BF16)
    product = exchange(product.reshape(-1, own, reals), (X, ZH, Y, ZL))
    return jnp.sum(product.astype(F32), axis=0)


def solution(mesh):
    split = Mesh(mesh.devices.reshape(4, 2, 2, 8, 4), EVERY)
    every = P(EVERY, None)
    return jax.shard_map(
        per_device,
        mesh=split,
        in_specs=(P(None, (X, ZH, CO), CELL), every, P(), P(None, CELL), P(), P()),
        out_specs=every,
        check_vma=False,
    )
```

```python
import functools

import jax
import jax.numpy as jnp
import ml_dtypes
import numpy as np
from jax import lax
from jax.experimental import pallas as pl
from jax.experimental.pallas import tpu as pltpu
from jax.sharding import Mesh
from jax.sharding import PartitionSpec as P

LSCALE = 4
GRID = 128
PARTS = 2
LOW = GRID // PARTS
X, ZH, CO, Y, ZL = "tm_0", "tm_1", "tm_2", "cell_0", "cell_1"
CELL = (Y, ZL)
EVERY = (X, ZH, CO, Y, ZL)
BF16 = jnp.bfloat16
F32 = jnp.float32
VMEM = pl.BlockSpec(memory_space=pltpu.VMEM)
SMEM = pl.BlockSpec(memory_space=pltpu.SMEM)


def halves(array):
    high = array.astype(np.float32).astype(ml_dtypes.bfloat16)
    return high, (array - high.astype(np.float64)).astype(np.float32).astype(ml_dtypes.bfloat16)


def spectrum():
    size = 2 * GRID
    gap = np.arange(GRID, dtype=np.float32)
    distance = np.sqrt(gap[:, None] * gap[:, None] + gap[None, :] * gap[None, :])
    table = (np.exp(-distance / np.float32(LSCALE)) / np.float32(8.0 * LSCALE)).astype(ml_dtypes.bfloat16)
    table = table.astype(np.float64)
    wave = np.concatenate([np.arange(GRID + 1), np.arange(1, GRID)])
    angle = 2.0 * np.pi * wave[:, None] * np.arange(GRID)[None, :] / size
    basis = np.where(np.arange(size)[:, None] <= GRID, np.cos(angle), np.sin(angle))
    edge = (wave == 0) | (wave == GRID)
    basis = basis * np.where(edge, np.sqrt(1.0 / size), np.sqrt(2.0 / size))[:, None]
    fold = np.cos(angle) * np.where(np.arange(GRID) == 0, 1.0, 2.0)[None, :]
    eigen = fold @ table @ fold.T
    high, low = halves(basis)
    return (
        np.concatenate([high.T, low.T], axis=0),
        np.concatenate([high, high], axis=1),
        low,
        np.concatenate([high.T, low.T], axis=0),
        np.concatenate([high, low], axis=1),
        eigen.astype(np.float32),
    )


def matmul(a, b):
    return jnp.dot(a, b, preferred_element_type=F32)


def parted(a):
    high = a.astype(BF16)
    return high, (a - high.astype(F32)).astype(BF16)


def hits(at, line):
    spread = jnp.broadcast_to(line.astype(F32), (16, line.shape[1])).astype(BF16)
    one = jnp.ones(spread.shape, BF16)
    zero = jnp.zeros(spread.shape, BF16)
    return [jnp.where(rows == spread, one, zero) for rows in at]


def spatial_kernel(lot, kept, which_ref, weight_ref, field_ref, rows_ref, cols_ref,
                   side_tall, basis_twice, basis_low, side_both, basis_wide, eigen_ref, out_ref, mixed, grid):
    times, chunks, _ = field_ref.shape
    pair = 2
    which = which_ref[0]
    strides = times // kept

    def mix(j, carry):
        rows = pl.ds(pl.multiple_of(j * 16, 16), 16)
        totals = [None] * kept
        for k in range(times):
            t = (k % (times // pair)) * pair + k // (times // pair)
            value = field_ref[k, rows, :].astype(F32)
            for s in range(kept):
                term = weight_ref[s * strides + which, t] * value
                totals[s] = term if k == 0 else totals[s] + term
        for s in range(kept):
            mixed[s, rows, :] = totals[s].astype(BF16).astype(F32)
        return carry

    lax.fori_loop(0, chunks // 16, mix, 0)
    grid[...] = jnp.zeros_like(grid)
    first_at = lax.broadcasted_iota(jnp.int32, (16, GRID), 0).astype(F32)
    wide_at = [(first_at + float(k)).astype(BF16) for k in range(0, PARTS * GRID, 16)]
    low_at = wide_at[: LOW // 16]

    def put(j, carry):
        first = pl.multiple_of(j * lot, lot)
        values = [mixed[s, pl.ds(first, lot), :] for s in range(kept)]
        rows = rows_ref[pl.ds(first, lot), :]
        low = rows % LOW
        wide = (rows // LOW) * GRID + cols_ref[pl.ds(first, lot), :]
        lefts = []
        rights = []
        for g in range(lot):
            low_hit = hits(low_at, low[g : g + 1, :])
            lines = [jnp.broadcast_to(v[g : g + 1, :], (16, GRID)).astype(BF16) for v in values]
            lefts.append(jnp.concatenate([hit * line for line in lines for hit in low_hit], axis=0))
            rights.append(jnp.concatenate(hits(wide_at, wide[g : g + 1, :]), axis=0))
        grid[...] += lax.dot_general(
            jnp.concatenate(lefts, axis=1),
            jnp.concatenate(rights, axis=1),
            (((1,), (1,)), ((), ())),
            preferred_element_type=F32,
        )
        return carry

    lax.fori_loop(0, chunks // lot, put, 0)
    whole = jnp.concatenate(
        [
            grid[s * LOW : (s + 1) * LOW, p * GRID : (p + 1) * GRID]
            for s in range(kept)
            for p in range(PARTS)
        ],
        axis=0,
    ).astype(BF16)
    ahead = matmul(jnp.concatenate([whole, whole], axis=1), side_tall[...])
    backs = []
    for s in range(kept):
        high, rest = parted(ahead[s * GRID : (s + 1) * GRID])
        waves = matmul(basis_twice[...], jnp.concatenate([high, rest], axis=0)) + matmul(basis_low[...], high)
        high, rest = parted(waves * eigen_ref[...])
        both = matmul(side_both[...], high)
        backs.append(both[:GRID] + (both[GRID:] + matmul(side_both[:GRID, :], rest)))
    high, rest = parted(jnp.concatenate(backs, axis=0))
    both = matmul(high, basis_wide[...])
    smooth = both[:, :GRID] + (both[:, GRID:] + matmul(rest, basis_wide[:, :GRID]))
    for s in range(kept):
        for p in range(PARTS):
            top = s * GRID + p * LOW
            grid[s * LOW : (s + 1) * LOW, p * GRID : (p + 1) * GRID] = smooth[top : top + LOW]
    weighted = grid[...].astype(BF16)

    line_at = lax.broadcasted_iota(jnp.int32, (LOW, GRID), 0)

    def take(j, carry):
        first = pl.multiple_of(j * lot, lot)
        rows = rows_ref[pl.ds(first, lot), :]
        low = rows % LOW
        wide = (rows // LOW) * GRID + cols_ref[pl.ds(first, lot), :]
        rights = [jnp.concatenate(hits(wide_at, wide[g : g + 1, :]), axis=0) for g in range(lot)]
        picked = matmul(weighted, jnp.concatenate(rights, axis=1))
        hit = [line_at == low[g : g + 1, :] for g in range(lot)]
        for s in range(kept):
            lines = []
            for g in range(lot):
                block = picked[s * LOW : (s + 1) * LOW, g * GRID : (g + 1) * GRID]
                lines.append(jnp.sum(jnp.where(hit[g], block, 0.0), axis=0, keepdims=True))
            span = pl.ds(pl.multiple_of(s * chunks + first, lot), lot)
            out_ref[span, :] = jnp.concatenate(lines, axis=0).astype(BF16)
        return carry

    lax.fori_loop(0, chunks // lot, take, 0)


def spatial(which, weight, field, rows, cols, kept):
    chunks = field.shape[1]
    constants = [jnp.asarray(c) for c in spectrum()]
    return pl.pallas_call(
        functools.partial(spatial_kernel, 64, kept),
        out_shape=jax.ShapeDtypeStruct((kept * chunks, GRID), BF16),
        in_specs=[SMEM] * 2 + [VMEM] * (3 + len(constants)),
        out_specs=VMEM,
        scratch_shapes=[
            pltpu.VMEM((kept, chunks, GRID), F32),
            pltpu.VMEM((kept * LOW, PARTS * GRID), F32),
        ],
        compiler_params=pltpu.CompilerParams(vmem_limit_bytes=48 << 20),
        cost_estimate=pl.CostEstimate(flops=10**10, bytes_accessed=18 << 20, transcendentals=0),
    )(which, weight, field, rows, cols, *constants)


def opening_kernel(half_ref, duals_ref, coords_ref, out_ref):
    width = coords_ref.shape[1]
    picked = jnp.where(half_ref[0] == 0, coords_ref[0:1, :], coords_ref[1:2, :]).astype(F32)
    lines = [picked[:, k : k + GRID] for k in range(0, width, GRID)]
    block = jnp.concatenate([duals_ref[...].astype(F32), *lines], axis=0).astype(BF16)
    out_ref[...] = jnp.broadcast_to(block, out_ref.shape)


def opening(half, duals, coords, count):
    rows = duals.shape[0] + coords.shape[1] // GRID
    return pl.pallas_call(
        opening_kernel,
        out_shape=jax.ShapeDtypeStruct((count, rows, GRID), BF16),
        in_specs=[SMEM, VMEM, VMEM],
        out_specs=VMEM,
    )(half, duals, coords)


def picking_kernel(here_ref, core_ref, owner_ref, time_ref, flat_ref, out_ref):
    count = owner_ref.shape[0]
    pair = 2
    lane = lax.broadcasted_iota(jnp.int32, (1, GRID), 1)
    ids = [jnp.where(time_ref[k : k + 1, :] >= here_ref[0], lane + k * GRID, -1) for k in range(count)]
    ids = jnp.concatenate(ids, axis=1).astype(F32)
    owners = owner_ref[...].astype(F32)
    first = core_ref[0] == 0
    order = []
    for side in range(pair):
        for k in range(0, count, pair):
            other, same = owners[k + 1 - side : k + 2 - side], owners[k + side : k + side + 1]
            order.append(jnp.where(first, other, same))
    slots = jnp.concatenate(order, axis=0).T
    flat = flat_ref[...]
    for k in range(count):
        chosen = jnp.where(slots[:, k : k + 1] == ids, 1.0, 0.0).astype(BF16)
        out_ref[k * GRID : (k + 1) * GRID, :] = matmul(chosen, flat).astype(BF16)


def picking(here, core, obs_owner, obs_time, flat):
    return pl.pallas_call(
        picking_kernel,
        out_shape=jax.ShapeDtypeStruct(flat.shape, BF16),
        in_specs=[SMEM] * 2 + [VMEM] * 3,
        out_specs=VMEM,
        compiler_params=pltpu.CompilerParams(vmem_limit_bytes=24 << 20),
        cost_estimate=pl.CostEstimate(flops=2 * flat.size * flat.shape[0], bytes_accessed=4 * flat.size, transcendentals=0),
    )(here, core, obs_owner.reshape(-1, GRID), obs_time.reshape(-1, GRID), flat)


def adjoint_kernel(here_ref, time_ref, duals_ref, flat_ref, out_ref):
    pair, groups, rows, reals = duals_ref.shape
    outer, again, part, folds, _ = out_ref.shape
    times = time_ref[...].astype(F32).T
    here = here_ref[0].astype(F32)
    seen = []
    for k in range(pair * groups):
        block = duals_ref[k % pair, k // pair].astype(F32)
        seen.append(jnp.where(times[:, k : k + 1] >= here, block, 0.0).astype(BF16))
    total = lax.dot_general(
        jnp.concatenate(seen, axis=0), flat_ref[...], (((0,), (0,)), ((), ())), preferred_element_type=F32
    )
    pieces = jnp.stack([total[:, k * GRID : (k + 1) * GRID] for k in range(folds)], axis=1).astype(BF16)
    for i in range(outer):
        for j in range(again):
            out_ref[i, j] = pieces[i * part : (i + 1) * part]


def adjoint(here, obs_time, duals, flat, outer, again):
    rows, reals = duals.shape[2:]
    return pl.pallas_call(
        adjoint_kernel,
        out_shape=jax.ShapeDtypeStruct((outer, again, reals // outer, flat.shape[1] // GRID, GRID), BF16),
        in_specs=[SMEM] + [VMEM] * 3,
        out_specs=VMEM,
        compiler_params=pltpu.CompilerParams(vmem_limit_bytes=24 << 20),
    )(here, obs_time.reshape(-1, rows), duals, flat)


def exchange(pieces, axes):
    return lax.all_to_all(pieces, axes, split_axis=0, concat_axis=0, tiled=True)


def copies(array, axes):
    return exchange(jnp.broadcast_to(array, (lax.axis_size(axes), *array.shape)), axes)


def per_device(sensitivity, duals, time_cov, cell_coords, obs_time, obs_owner):
    obs = sensitivity.shape[0]
    own, reals = duals.shape
    flat = sensitivity.reshape(obs, -1)
    here = lax.axis_index((X, ZH, CO)).reshape(1)
    core = lax.axis_index(CO).reshape(1)
    nx, nh, pair = (lax.axis_size(a) for a in (X, ZH, CO))
    which = lax.axis_index((ZH, CO)).reshape(1)

    plane = (ZH, Y, ZL)
    first = opening(lax.axis_index(ZH).reshape(1), duals, cell_coords, lax.axis_size(plane))
    even = core[0] == 0
    first, here, core, which, even = lax.optimization_barrier((first, here, core, which, even))
    first = exchange(first, plane)
    coords = first[:, own:].reshape(nh, -1, GRID).astype(jnp.int32)
    second = copies(first[:, :own].reshape(-1, reals), X)
    third = lax.all_gather(second.reshape(nx * nh, -1, reals), CO, axis=0)
    pieces = adjoint(here, obs_time, third, flat, nx, nh)
    pieces, owner = lax.optimization_barrier((pieces, obs_owner))
    field = exchange(pieces.reshape(-1, *pieces.shape[3:]), (X, ZH, Y, ZL))
    picked = picking(here, core, owner, obs_time, flat)
    field, picked = lax.optimization_barrier((field, picked))
    field = lax.all_gather(field.reshape(nx * nh, -1, GRID), CO, axis=0, tiled=True)

    weighted = spatial(which, time_cov, field, coords[0], coords[1], nx)
    weighted = exchange(weighted.reshape(reals, -1, GRID), (X, Y, ZL)).reshape(reals, -1)
    theirs, ours = (
        lax.dot_general(rows, weighted, (((1,), (1,)), ((), ())), preferred_element_type=F32)
        for rows in jnp.split(picked, pair)
    )
    swapped = lax.all_gather(theirs.astype(BF16), CO, axis=0)
    got = jnp.where(even, swapped[1], swapped[0])
    product = (ours + got.astype(F32)).astype(BF16)
    product = exchange(product.reshape(-1, own, reals), (X, ZH, Y, ZL))
    return jnp.sum(product.astype(F32), axis=0)


def solution(mesh):
    split = Mesh(mesh.devices.reshape(4, 2, 2, 8, 4), EVERY)
    every = P(EVERY, None)
    return jax.shard_map(
        per_device,
        mesh=split,
        in_specs=(P(None, (X, ZH, CO), CELL), every, P(), P(None, CELL), P(), P()),
        out_specs=every,
        check_vma=False,
    )
```

```python
import functools

import jax
import jax.numpy as jnp
import ml_dtypes
import numpy as np
from jax import lax
from jax.experimental import pallas as pl
from jax.experimental.pallas import tpu as pltpu
from jax.sharding import Mesh
from jax.sharding import PartitionSpec as P

LSCALE = 4
GRID = 128
PARTS = 2
LOW = GRID // PARTS
X, ZH, CO, Y, ZL = "tm_0", "tm_1", "tm_2", "cell_0", "cell_1"
CELL = (Y, ZL)
EVERY = (X, ZH, CO, Y, ZL)
BF16 = jnp.bfloat16
F32 = jnp.float32
VMEM = pl.BlockSpec(memory_space=pltpu.VMEM)
SMEM = pl.BlockSpec(memory_space=pltpu.SMEM)


def halves(array):
    high = array.astype(np.float32).astype(ml_dtypes.bfloat16)
    return high, (array - high.astype(np.float64)).astype(np.float32).astype(ml_dtypes.bfloat16)


def spectrum():
    size = 2 * GRID
    gap = np.arange(GRID, dtype=np.float32)
    distance = np.sqrt(gap[:, None] * gap[:, None] + gap[None, :] * gap[None, :])
    table = (np.exp(-distance / np.float32(LSCALE)) / np.float32(8.0 * LSCALE)).astype(ml_dtypes.bfloat16)
    table = table.astype(np.float64)
    wave = np.concatenate([np.arange(GRID + 1), np.arange(1, GRID)])
    angle = 2.0 * np.pi * wave[:, None] * np.arange(GRID)[None, :] / size
    basis = np.where(np.arange(size)[:, None] <= GRID, np.cos(angle), np.sin(angle))
    edge = (wave == 0) | (wave == GRID)
    basis = basis * np.where(edge, np.sqrt(1.0 / size), np.sqrt(2.0 / size))[:, None]
    fold = np.cos(angle) * np.where(np.arange(GRID) == 0, 1.0, 2.0)[None, :]
    eigen = fold @ table @ fold.T
    high, low = halves(basis)
    return (
        np.concatenate([high.T, low.T], axis=0),
        np.concatenate([high, high], axis=1),
        low,
        np.concatenate([high.T, low.T], axis=0),
        np.concatenate([high, low], axis=1),
        eigen.astype(np.float32),
    )


def matmul(a, b):
    return jnp.dot(a, b, preferred_element_type=F32)


def parted(a):
    high = a.astype(BF16)
    return high, (a - high.astype(F32)).astype(BF16)


def hits(at, line):
    spread = jnp.broadcast_to(line.astype(F32), (16, line.shape[1])).astype(BF16)
    one = jnp.ones(spread.shape, BF16)
    zero = jnp.zeros(spread.shape, BF16)
    return [jnp.where(rows == spread, one, zero) for rows in at]


def spatial_kernel(lot, kept, which_ref, weight_ref, field_ref, rows_ref, cols_ref,
                   side_tall, basis_twice, basis_low, side_both, basis_wide, eigen_ref, out_ref, mixed, grid):
    times, chunks, _ = field_ref.shape
    pair = 2
    which = which_ref[0]
    strides = times // kept

    def mix(j, carry):
        rows = pl.ds(pl.multiple_of(j * 32, 32), 32)
        totals = [None] * kept
        for k in range(times):
            t = (k % (times // pair)) * pair + k // (times // pair)
            value = field_ref[k, rows, :].astype(F32)
            for s in range(kept):
                term = weight_ref[s * strides + which, t] * value
                totals[s] = term if k == 0 else totals[s] + term
        for s in range(kept):
            mixed[s, rows, :] = totals[s].astype(BF16).astype(F32)
        return carry

    lax.fori_loop(0, chunks // 32, mix, 0)
    grid[...] = jnp.zeros_like(grid)
    first_at = lax.broadcasted_iota(jnp.int32, (16, GRID), 0).astype(F32)
    wide_at = [(first_at + float(k)).astype(BF16) for k in range(0, PARTS * GRID, 16)]
    low_at = wide_at[: LOW // 16]

    def put(j, carry):
        first = pl.multiple_of(j * lot, lot)
        values = [mixed[s, pl.ds(first, lot), :] for s in range(kept)]
        rows = rows_ref[pl.ds(first, lot), :]
        low = rows % LOW
        wide = (rows // LOW) * GRID + cols_ref[pl.ds(first, lot), :]
        lefts = []
        rights = []
        for g in range(lot):
            low_hit = hits(low_at, low[g : g + 1, :])
            lines = [jnp.broadcast_to(v[g : g + 1, :], (16, GRID)).astype(BF16) for v in values]
            lefts.append(jnp.concatenate([hit * line for line in lines for hit in low_hit], axis=0))
            rights.append(jnp.concatenate(hits(wide_at, wide[g : g + 1, :]), axis=0))
        grid[...] += lax.dot_general(
            jnp.concatenate(lefts, axis=1),
            jnp.concatenate(rights, axis=1),
            (((1,), (1,)), ((), ())),
            preferred_element_type=F32,
        )
        return carry

    lax.fori_loop(0, chunks // lot, put, 0)
    whole = jnp.concatenate(
        [
            grid[s * LOW : (s + 1) * LOW, p * GRID : (p + 1) * GRID]
            for s in range(kept)
            for p in range(PARTS)
        ],
        axis=0,
    ).astype(BF16)
    ahead = matmul(jnp.concatenate([whole, whole], axis=1), side_tall[...])
    backs = []
    for s in range(kept):
        high, rest = parted(ahead[s * GRID : (s + 1) * GRID])
        waves = matmul(basis_twice[...], jnp.concatenate([high, rest], axis=0)) + matmul(basis_low[...], high)
        high, rest = parted(waves * eigen_ref[...])
        both = matmul(side_both[...], high)
        backs.append(both[:GRID] + (both[GRID:] + matmul(side_both[:GRID, :], rest)))
    high, rest = parted(jnp.concatenate(backs, axis=0))
    both = matmul(high, basis_wide[...])
    smooth = both[:, :GRID] + (both[:, GRID:] + matmul(rest, basis_wide[:, :GRID]))
    for s in range(kept):
        for p in range(PARTS):
            top = s * GRID + p * LOW
            grid[s * LOW : (s + 1) * LOW, p * GRID : (p + 1) * GRID] = smooth[top : top + LOW]
    weighted = grid[...].astype(BF16)

    line_at = lax.broadcasted_iota(jnp.int32, (LOW, GRID), 0)

    def take(j, carry):
        first = pl.multiple_of(j * lot, lot)
        rows = rows_ref[pl.ds(first, lot), :]
        low = rows % LOW
        wide = (rows // LOW) * GRID + cols_ref[pl.ds(first, lot), :]
        rights = [jnp.concatenate(hits(wide_at, wide[g : g + 1, :]), axis=0) for g in range(lot)]
        picked = matmul(weighted, jnp.concatenate(rights, axis=1))
        hit = [line_at == low[g : g + 1, :] for g in range(lot)]
        for s in range(kept):
            lines = []
            for g in range(lot):
                block = picked[s * LOW : (s + 1) * LOW, g * GRID : (g + 1) * GRID]
                lines.append(jnp.sum(jnp.where(hit[g], block, 0.0), axis=0, keepdims=True))
            span = pl.ds(pl.multiple_of(s * chunks + first, lot), lot)
            out_ref[span, :] = jnp.concatenate(lines, axis=0).astype(BF16)
        return carry

    lax.fori_loop(0, chunks // lot, take, 0)


def spatial(which, weight, field, rows, cols, kept):
    chunks = field.shape[1]
    constants = [jnp.asarray(c) for c in spectrum()]
    return pl.pallas_call(
        functools.partial(spatial_kernel, 64, kept),
        out_shape=jax.ShapeDtypeStruct((kept * chunks, GRID), BF16),
        in_specs=[SMEM] * 2 + [VMEM] * (3 + len(constants)),
        out_specs=VMEM,
        scratch_shapes=[
            pltpu.VMEM((kept, chunks, GRID), F32),
            pltpu.VMEM((kept * LOW, PARTS * GRID), F32),
        ],
        compiler_params=pltpu.CompilerParams(vmem_limit_bytes=48 << 20),
        cost_estimate=pl.CostEstimate(flops=10**10, bytes_accessed=18 << 20, transcendentals=0),
    )(which, weight, field, rows, cols, *constants)


def opening_kernel(half_ref, duals_ref, coords_ref, out_ref):
    width = coords_ref.shape[1]
    picked = jnp.where(half_ref[0] == 0, coords_ref[0:1, :], coords_ref[1:2, :]).astype(F32)
    lines = [picked[:, k : k + GRID] for k in range(0, width, GRID)]
    block = jnp.concatenate([duals_ref[...].astype(F32), *lines], axis=0).astype(BF16)
    out_ref[...] = jnp.broadcast_to(block, out_ref.shape)


def opening(half, duals, coords, count):
    rows = duals.shape[0] + coords.shape[1] // GRID
    return pl.pallas_call(
        opening_kernel,
        out_shape=jax.ShapeDtypeStruct((count, rows, GRID), BF16),
        in_specs=[SMEM, VMEM, VMEM],
        out_specs=VMEM,
    )(half, duals, coords)


def picking_kernel(here_ref, core_ref, owner_ref, time_ref, flat_ref, out_ref):
    count = owner_ref.shape[0]
    pair = 2
    lane = lax.broadcasted_iota(jnp.int32, (1, GRID), 1)
    ids = [jnp.where(time_ref[k : k + 1, :] >= here_ref[0], lane + k * GRID, -1) for k in range(count)]
    ids = jnp.concatenate(ids, axis=1).astype(F32)
    owners = owner_ref[...].astype(F32)
    first = core_ref[0] == 0
    order = []
    for side in range(pair):
        for k in range(0, count, pair):
            other, same = owners[k + 1 - side : k + 2 - side], owners[k + side : k + side + 1]
            order.append(jnp.where(first, other, same))
    slots = jnp.concatenate(order, axis=0).T
    flat = flat_ref[...]
    for k in range(count):
        chosen = jnp.where(slots[:, k : k + 1] == ids, 1.0, 0.0).astype(BF16)
        out_ref[k * GRID : (k + 1) * GRID, :] = matmul(chosen, flat).astype(BF16)


def picking(here, core, obs_owner, obs_time, flat):
    return pl.pallas_call(
        picking_kernel,
        out_shape=jax.ShapeDtypeStruct(flat.shape, BF16),
        in_specs=[SMEM] * 2 + [VMEM] * 3,
        out_specs=VMEM,
        compiler_params=pltpu.CompilerParams(vmem_limit_bytes=24 << 20),
        cost_estimate=pl.CostEstimate(flops=2 * flat.size * flat.shape[0], bytes_accessed=4 * flat.size, transcendentals=0),
    )(here, core, obs_owner.reshape(-1, GRID), obs_time.reshape(-1, GRID), flat)


def adjoint_kernel(here_ref, time_ref, duals_ref, flat_ref, out_ref):
    pair, groups, rows, reals = duals_ref.shape
    outer, again, part, folds, _ = out_ref.shape
    keep = jnp.where(time_ref[...] >= here_ref[0], 1.0, 0.0).T
    seen = []
    for k in range(pair * groups):
        column = jnp.broadcast_to(keep[:, k : k + 1], (rows, reals)).astype(BF16)
        seen.append(duals_ref[k % pair, k // pair] * column)
    total = lax.dot_general(
        jnp.concatenate(seen, axis=0), flat_ref[...], (((0,), (0,)), ((), ())), preferred_element_type=F32
    )
    pieces = total.reshape(reals, folds, GRID).astype(BF16)
    for i in range(outer):
        for j in range(again):
            out_ref[i, j] = pieces[i * part : (i + 1) * part]


def adjoint(here, obs_time, duals, flat, outer, again):
    rows, reals = duals.shape[2:]
    return pl.pallas_call(
        adjoint_kernel,
        out_shape=jax.ShapeDtypeStruct((outer, again, reals // outer, flat.shape[1] // GRID, GRID), BF16),
        in_specs=[SMEM] + [VMEM] * 3,
        out_specs=VMEM,
        compiler_params=pltpu.CompilerParams(vmem_limit_bytes=24 << 20),
    )(here, obs_time.reshape(-1, rows), duals, flat)


def exchange(pieces, axes):
    return lax.all_to_all(pieces, axes, split_axis=0, concat_axis=0, tiled=True)


def copies(array, axes):
    return exchange(jnp.broadcast_to(array, (lax.axis_size(axes), *array.shape)), axes)


def per_device(sensitivity, duals, time_cov, cell_coords, obs_time, obs_owner):
    obs = sensitivity.shape[0]
    own, reals = duals.shape
    flat = sensitivity.reshape(obs, -1)
    here = lax.axis_index((X, ZH, CO)).reshape(1)
    core = lax.axis_index(CO).reshape(1)
    nx, nh, pair = (lax.axis_size(a) for a in (X, ZH, CO))
    which = lax.axis_index((ZH, CO)).reshape(1)

    plane = (ZH, Y, ZL)
    first = opening(lax.axis_index(ZH).reshape(1), duals, cell_coords, lax.axis_size(plane))
    even = core[0] == 0
    first, here, core, which, even = lax.optimization_barrier((first, here, core, which, even))
    first = exchange(first, plane)
    coords = first[:, own:].reshape(nh, -1, GRID).astype(jnp.int32)
    second = copies(first[:, :own].reshape(-1, reals), X)
    third = lax.all_gather(second.reshape(nx * nh, -1, reals), CO, axis=0)
    pieces = adjoint(here, obs_time, third, flat, nx, nh)
    pieces, owner = lax.optimization_barrier((pieces, obs_owner))
    field = exchange(pieces.reshape(-1, *pieces.shape[3:]), (X, ZH, Y, ZL))
    picked = picking(here, core, owner, obs_time, flat)
    field, picked = lax.optimization_barrier((field, picked))
    field = lax.all_gather(field.reshape(nx * nh, -1, GRID), CO, axis=0, tiled=True)

    weighted = spatial(which, time_cov, field, coords[0], coords[1], nx)
    weighted = exchange(weighted.reshape(reals, -1, GRID), (X, Y, ZL)).reshape(reals, -1)
    theirs, ours = (
        lax.dot_general(rows, weighted, (((1,), (1,)), ((), ())), preferred_element_type=F32)
        for rows in jnp.split(picked, pair)
    )
    swapped = lax.all_gather(theirs.astype(BF16), CO, axis=0)
    got = jnp.where(even, swapped[1], swapped[0])
    product = (ours + got.astype(F32)).astype(BF16)
    product = exchange(product.reshape(-1, own, reals), (X, ZH, Y, ZL))
    return jnp.sum(product.astype(F32), axis=0)


def solution(mesh):
    split = Mesh(mesh.devices.reshape(4, 2, 2, 8, 4), EVERY)
    every = P(EVERY, None)
    return jax.shard_map(
        per_device,
        mesh=split,
        in_specs=(P(None, (X, ZH, CO), CELL), every, P(), P(None, CELL), P(), P()),
        out_specs=every,
        check_vma=False,
    )
```

```python
import functools

import jax
import jax.numpy as jnp
import ml_dtypes
import numpy as np
from jax import lax
from jax.experimental import pallas as pl
from jax.experimental.pallas import tpu as pltpu
from jax.sharding import Mesh
from jax.sharding import PartitionSpec as P

LSCALE = 4
GRID = 128
PARTS = 2
LOW = GRID // PARTS
X, ZH, CO, Y, ZL = "tm_0", "tm_1", "tm_2", "cell_0", "cell_1"
CELL = (Y, ZL)
EVERY = (X, ZH, CO, Y, ZL)
BF16 = jnp.bfloat16
F32 = jnp.float32
VMEM = pl.BlockSpec(memory_space=pltpu.VMEM)
SMEM = pl.BlockSpec(memory_space=pltpu.SMEM)


def halves(array):
    high = array.astype(np.float32).astype(ml_dtypes.bfloat16)
    return high, (array - high.astype(np.float64)).astype(np.float32).astype(ml_dtypes.bfloat16)


def spectrum():
    size = 2 * GRID
    gap = np.arange(GRID, dtype=np.float32)
    distance = np.sqrt(gap[:, None] * gap[:, None] + gap[None, :] * gap[None, :])
    table = (np.exp(-distance / np.float32(LSCALE)) / np.float32(8.0 * LSCALE)).astype(ml_dtypes.bfloat16)
    table = table.astype(np.float64)
    wave = np.concatenate([np.arange(GRID + 1), np.arange(1, GRID)])
    angle = 2.0 * np.pi * wave[:, None] * np.arange(GRID)[None, :] / size
    basis = np.where(np.arange(size)[:, None] <= GRID, np.cos(angle), np.sin(angle))
    edge = (wave == 0) | (wave == GRID)
    basis = basis * np.where(edge, np.sqrt(1.0 / size), np.sqrt(2.0 / size))[:, None]
    fold = np.cos(angle) * np.where(np.arange(GRID) == 0, 1.0, 2.0)[None, :]
    eigen = fold @ table @ fold.T
    high, low = halves(basis)
    return (
        np.concatenate([high.T, low.T], axis=0),
        np.concatenate([high, high], axis=1),
        low,
        np.concatenate([high.T, low.T], axis=0),
        np.concatenate([high, low], axis=1),
        eigen.astype(np.float32),
    )


def matmul(a, b):
    return jnp.dot(a, b, preferred_element_type=F32)


def parted(a):
    high = a.astype(BF16)
    return high, (a - high.astype(F32)).astype(BF16)


def hits(at, line):
    spread = jnp.broadcast_to(line.astype(F32), (16, line.shape[1])).astype(BF16)
    one = jnp.ones(spread.shape, BF16)
    zero = jnp.zeros(spread.shape, BF16)
    return [jnp.where(rows == spread, one, zero) for rows in at]


def spatial_kernel(lot, kept, which_ref, weight_ref, field_ref, rows_ref, cols_ref,
                   side_tall, basis_twice, basis_low, side_both, basis_wide, eigen_ref, out_ref, mixed, grid):
    times, chunks, _ = field_ref.shape
    pair = 2
    which = which_ref[0]
    strides = times // kept

    picked = [weight_ref[pl.ds(s * strides + which, 1), :] for s in range(kept)]

    def mix(j, carry):
        rows = pl.ds(pl.multiple_of(j * 32, 32), 32)
        totals = [None] * kept
        for k in range(times):
            t = (k % (times // pair)) * pair + k // (times // pair)
            value = field_ref[k, rows, :].astype(F32)
            for s in range(kept):
                term = jnp.broadcast_to(picked[s][:, t : t + 1], value.shape) * value
                totals[s] = term if k == 0 else totals[s] + term
        for s in range(kept):
            mixed[s, rows, :] = totals[s].astype(BF16).astype(F32)
        return carry

    lax.fori_loop(0, chunks // 32, mix, 0)
    grid[...] = jnp.zeros_like(grid)
    first_at = lax.broadcasted_iota(jnp.int32, (16, GRID), 0).astype(F32)
    wide_at = [(first_at + float(k)).astype(BF16) for k in range(0, PARTS * GRID, 16)]
    low_at = wide_at[: LOW // 16]

    def put(j, carry):
        first = pl.multiple_of(j * lot, lot)
        values = [mixed[s, pl.ds(first, lot), :] for s in range(kept)]
        rows = rows_ref[pl.ds(first, lot), :]
        low = rows % LOW
        wide = (rows // LOW) * GRID + cols_ref[pl.ds(first, lot), :]
        lefts = []
        rights = []
        for g in range(lot):
            low_hit = hits(low_at, low[g : g + 1, :])
            lines = [jnp.broadcast_to(v[g : g + 1, :], (16, GRID)).astype(BF16) for v in values]
            lefts.append(jnp.concatenate([hit * line for line in lines for hit in low_hit], axis=0))
            rights.append(jnp.concatenate(hits(wide_at, wide[g : g + 1, :]), axis=0))
        grid[...] += lax.dot_general(
            jnp.concatenate(lefts, axis=1),
            jnp.concatenate(rights, axis=1),
            (((1,), (1,)), ((), ())),
            preferred_element_type=F32,
        )
        return carry

    lax.fori_loop(0, chunks // lot, put, 0)
    whole = jnp.concatenate(
        [
            grid[s * LOW : (s + 1) * LOW, p * GRID : (p + 1) * GRID]
            for s in range(kept)
            for p in range(PARTS)
        ],
        axis=0,
    ).astype(BF16)
    ahead = matmul(jnp.concatenate([whole, whole], axis=1), side_tall[...])
    backs = []
    for s in range(kept):
        high, rest = parted(ahead[s * GRID : (s + 1) * GRID])
        waves = matmul(basis_twice[...], jnp.concatenate([high, rest], axis=0)) + matmul(basis_low[...], high)
        high, rest = parted(waves * eigen_ref[...])
        both = matmul(side_both[...], high)
        backs.append(both[:GRID] + (both[GRID:] + matmul(side_both[:GRID, :], rest)))
    high, rest = parted(jnp.concatenate(backs, axis=0))
    both = matmul(high, basis_wide[...])
    smooth = both[:, :GRID] + (both[:, GRID:] + matmul(rest, basis_wide[:, :GRID]))
    for s in range(kept):
        for p in range(PARTS):
            top = s * GRID + p * LOW
            grid[s * LOW : (s + 1) * LOW, p * GRID : (p + 1) * GRID] = smooth[top : top + LOW]
    weighted = grid[...].astype(BF16)

    line_at = lax.broadcasted_iota(jnp.int32, (LOW, GRID), 0)

    def take(j, carry):
        first = pl.multiple_of(j * lot, lot)
        rows = rows_ref[pl.ds(first, lot), :]
        low = rows % LOW
        wide = (rows // LOW) * GRID + cols_ref[pl.ds(first, lot), :]
        rights = [jnp.concatenate(hits(wide_at, wide[g : g + 1, :]), axis=0) for g in range(lot)]
        picked = matmul(weighted, jnp.concatenate(rights, axis=1))
        hit = [line_at == low[g : g + 1, :] for g in range(lot)]
        for s in range(kept):
            lines = []
            for g in range(lot):
                block = picked[s * LOW : (s + 1) * LOW, g * GRID : (g + 1) * GRID]
                lines.append(jnp.sum(jnp.where(hit[g], block, 0.0), axis=0, keepdims=True))
            span = pl.ds(pl.multiple_of(s * chunks + first, lot), lot)
            out_ref[span, :] = jnp.concatenate(lines, axis=0).astype(BF16)
        return carry

    lax.fori_loop(0, chunks // lot, take, 0)


def spatial(which, weight, field, rows, cols, kept):
    chunks = field.shape[1]
    constants = [jnp.asarray(c) for c in spectrum()]
    return pl.pallas_call(
        functools.partial(spatial_kernel, 64, kept),
        out_shape=jax.ShapeDtypeStruct((kept * chunks, GRID), BF16),
        in_specs=[SMEM] + [VMEM] * (4 + len(constants)),
        out_specs=VMEM,
        scratch_shapes=[
            pltpu.VMEM((kept, chunks, GRID), F32),
            pltpu.VMEM((kept * LOW, PARTS * GRID), F32),
        ],
        compiler_params=pltpu.CompilerParams(vmem_limit_bytes=48 << 20),
        cost_estimate=pl.CostEstimate(flops=10**10, bytes_accessed=18 << 20, transcendentals=0),
    )(which, weight, field, rows, cols, *constants)


def opening_kernel(half_ref, duals_ref, coords_ref, out_ref):
    width = coords_ref.shape[1]
    picked = jnp.where(half_ref[0] == 0, coords_ref[0:1, :], coords_ref[1:2, :]).astype(F32)
    lines = [picked[:, k : k + GRID] for k in range(0, width, GRID)]
    block = jnp.concatenate([duals_ref[...].astype(F32), *lines], axis=0).astype(BF16)
    out_ref[...] = jnp.broadcast_to(block, out_ref.shape)


def opening(half, duals, coords, count):
    rows = duals.shape[0] + coords.shape[1] // GRID
    return pl.pallas_call(
        opening_kernel,
        out_shape=jax.ShapeDtypeStruct((count, rows, GRID), BF16),
        in_specs=[SMEM, VMEM, VMEM],
        out_specs=VMEM,
        compiler_params=pltpu.CompilerParams(vmem_limit_bytes=2 << 20),
    )(half, duals, coords)


def picking_kernel(here_ref, core_ref, owner_ref, time_ref, flat_ref, out_ref):
    count = owner_ref.shape[0]
    pair = 2
    lane = lax.broadcasted_iota(jnp.int32, (1, GRID), 1)
    ids = [jnp.where(time_ref[k : k + 1, :] >= here_ref[0], lane + k * GRID, -1) for k in range(count)]
    ids = jnp.concatenate(ids, axis=1).astype(F32)
    owners = owner_ref[...].astype(F32)
    first = core_ref[0] == 0
    order = []
    for side in range(pair):
        for k in range(0, count, pair):
            other, same = owners[k + 1 - side : k + 2 - side], owners[k + side : k + side + 1]
            order.append(jnp.where(first, other, same))
    slots = jnp.concatenate(order, axis=0).T
    flat = flat_ref[...]
    for k in range(count):
        chosen = jnp.where(slots[:, k : k + 1] == ids, 1.0, 0.0).astype(BF16)
        out_ref[k * GRID : (k + 1) * GRID, :] = matmul(chosen, flat).astype(BF16)


def picking(here, core, obs_owner, obs_time, flat):
    return pl.pallas_call(
        picking_kernel,
        out_shape=jax.ShapeDtypeStruct(flat.shape, BF16),
        in_specs=[SMEM] * 2 + [VMEM] * 3,
        out_specs=VMEM,
        compiler_params=pltpu.CompilerParams(vmem_limit_bytes=24 << 20),
        cost_estimate=pl.CostEstimate(flops=2 * flat.size * flat.shape[0], bytes_accessed=4 * flat.size, transcendentals=0),
    )(here, core, obs_owner.reshape(-1, GRID), obs_time.reshape(-1, GRID), flat)


def adjoint_kernel(here_ref, time_ref, duals_ref, flat_ref, out_ref):
    pair, groups, rows, reals = duals_ref.shape
    outer, again, part, folds, _ = out_ref.shape
    keep = jnp.where(time_ref[...] >= here_ref[0], 1.0, 0.0).T
    seen = []
    for k in range(pair * groups):
        column = jnp.broadcast_to(keep[:, k : k + 1], (rows, reals)).astype(BF16)
        seen.append(duals_ref[k % pair, k // pair] * column)
    total = lax.dot_general(
        jnp.concatenate(seen, axis=0), flat_ref[...], (((0,), (0,)), ((), ())), preferred_element_type=F32
    )
    pieces = total.reshape(reals, folds, GRID).astype(BF16)
    for i in range(outer):
        for j in range(again):
            out_ref[i, j] = pieces[i * part : (i + 1) * part]


def adjoint(here, obs_time, duals, flat, outer, again):
    rows, reals = duals.shape[2:]
    return pl.pallas_call(
        adjoint_kernel,
        out_shape=jax.ShapeDtypeStruct((outer, again, reals // outer, flat.shape[1] // GRID, GRID), BF16),
        in_specs=[SMEM] + [VMEM] * 3,
        out_specs=VMEM,
        compiler_params=pltpu.CompilerParams(vmem_limit_bytes=24 << 20),
    )(here, obs_time.reshape(-1, rows), duals, flat)


def exchange(pieces, axes):
    return lax.all_to_all(pieces, axes, split_axis=0, concat_axis=0, tiled=True)


def copies(array, axes):
    return exchange(jnp.broadcast_to(array, (lax.axis_size(axes), *array.shape)), axes)


def per_device(sensitivity, duals, time_cov, cell_coords, obs_time, obs_owner):
    obs = sensitivity.shape[0]
    own, reals = duals.shape
    flat = sensitivity.reshape(obs, -1)
    here = lax.axis_index((X, ZH, CO)).reshape(1)
    core = lax.axis_index(CO).reshape(1)
    nx, nh, pair = (lax.axis_size(a) for a in (X, ZH, CO))
    which = lax.axis_index((ZH, CO)).reshape(1)

    plane = (ZH, Y, ZL)
    first = opening(lax.axis_index(ZH).reshape(1), duals, cell_coords, lax.axis_size(plane))
    even = core[0] == 0
    first, here, core, which, even = lax.optimization_barrier((first, here, core, which, even))
    first = exchange(first, plane)
    coords = first[:, own:].reshape(nh, -1, GRID).astype(jnp.int32)
    second = copies(first[:, :own].reshape(-1, reals), X)
    third = lax.all_gather(second.reshape(nx * nh, -1, reals), CO, axis=0)
    pieces = adjoint(here, obs_time, third, flat, nx, nh)
    pieces, owner = lax.optimization_barrier((pieces, obs_owner))
    field = exchange(pieces.reshape(-1, *pieces.shape[3:]), (X, ZH, Y, ZL))
    picked = picking(here, core, owner, obs_time, flat)
    field, picked = lax.optimization_barrier((field, picked))
    field = lax.all_gather(field.reshape(nx * nh, -1, GRID), CO, axis=0, tiled=True)

    weighted = spatial(which, time_cov, field, coords[0], coords[1], nx)
    weighted = exchange(weighted.reshape(reals, -1, GRID), (X, Y, ZL)).reshape(reals, -1)
    theirs, ours = (
        lax.dot_general(rows, weighted, (((1,), (1,)), ((), ())), preferred_element_type=F32)
        for rows in jnp.split(picked, pair)
    )
    swapped = lax.all_gather(theirs.astype(BF16), CO, axis=0)
    got = jnp.where(even, swapped[1], swapped[0])
    product = (ours + got.astype(F32)).astype(BF16)
    product = exchange(product.reshape(-1, own, reals), (X, ZH, Y, ZL))
    return jnp.sum(product.astype(F32), axis=0)


def solution(mesh):
    split = Mesh(mesh.devices.reshape(4, 2, 2, 8, 4), EVERY)
    every = P(EVERY, None)
    return jax.shard_map(
        per_device,
        mesh=split,
        in_specs=(P(None, (X, ZH, CO), CELL), every, P(), P(None, CELL), P(), P()),
        out_specs=every,
        check_vma=False,
    )
```

```python
import functools

import jax
import jax.numpy as jnp
import ml_dtypes
import numpy as np
from jax import lax
from jax.experimental import pallas as pl
from jax.experimental.pallas import tpu as pltpu
from jax.sharding import Mesh
from jax.sharding import PartitionSpec as P

LSCALE = 4
GRID = 128
PARTS = 2
LOW = GRID // PARTS
X, ZH, CO, Y, ZL = "tm_0", "tm_1", "tm_2", "cell_0", "cell_1"
CELL = (Y, ZL)
EVERY = (X, ZH, CO, Y, ZL)
BF16 = jnp.bfloat16
F32 = jnp.float32
VMEM = pl.BlockSpec(memory_space=pltpu.VMEM)
SMEM = pl.BlockSpec(memory_space=pltpu.SMEM)


def halves(array):
    high = array.astype(np.float32).astype(ml_dtypes.bfloat16)
    return high, (array - high.astype(np.float64)).astype(np.float32).astype(ml_dtypes.bfloat16)


def spectrum():
    size = 2 * GRID
    gap = np.arange(GRID, dtype=np.float32)
    distance = np.sqrt(gap[:, None] * gap[:, None] + gap[None, :] * gap[None, :])
    table = (np.exp(-distance / np.float32(LSCALE)) / np.float32(8.0 * LSCALE)).astype(ml_dtypes.bfloat16)
    table = table.astype(np.float64)
    wave = np.concatenate([np.arange(GRID + 1), np.arange(1, GRID)])
    angle = 2.0 * np.pi * wave[:, None] * np.arange(GRID)[None, :] / size
    basis = np.where(np.arange(size)[:, None] <= GRID, np.cos(angle), np.sin(angle))
    edge = (wave == 0) | (wave == GRID)
    basis = basis * np.where(edge, np.sqrt(1.0 / size), np.sqrt(2.0 / size))[:, None]
    fold = np.cos(angle) * np.where(np.arange(GRID) == 0, 1.0, 2.0)[None, :]
    eigen = fold @ table @ fold.T
    high, low = halves(basis)
    return (
        np.concatenate([high.T, low.T], axis=0),
        np.concatenate([high, high], axis=1),
        low,
        np.concatenate([high.T, low.T], axis=0),
        np.concatenate([high, low], axis=1),
        eigen.astype(np.float32),
    )


def matmul(a, b):
    return jnp.dot(a, b, preferred_element_type=F32)


def parted(a):
    high = a.astype(BF16)
    return high, (a - high.astype(F32)).astype(BF16)


def hits(at, line):
    spread = jnp.broadcast_to(line.astype(F32), (16, line.shape[1])).astype(BF16)
    one = jnp.ones(spread.shape, BF16)
    zero = jnp.zeros(spread.shape, BF16)
    return [jnp.where(rows == spread, one, zero) for rows in at]


def spatial_kernel(lot, kept, which_ref, weight_ref, field_ref, rows_ref, cols_ref,
                   side_tall, basis_twice, basis_low, side_both, basis_wide, eigen_ref, out_ref, mixed, grid):
    times, chunks, _ = field_ref.shape
    pair = 2
    which = which_ref[0]
    strides = times // kept

    picked = [weight_ref[pl.ds(s * strides + which, 1), :] for s in range(kept)]

    def mix(j, carry):
        rows = pl.ds(pl.multiple_of(j * 32, 32), 32)
        totals = [None] * kept
        for k in range(times):
            t = (k % (times // pair)) * pair + k // (times // pair)
            value = field_ref[k, rows, :].astype(F32)
            for s in range(kept):
                term = jnp.broadcast_to(picked[s][:, t : t + 1], value.shape) * value
                totals[s] = term if k == 0 else totals[s] + term
        for s in range(kept):
            mixed[s, rows, :] = totals[s].astype(BF16).astype(F32)
        return carry

    lax.fori_loop(0, chunks // 32, mix, 0)
    grid[...] = jnp.zeros_like(grid)
    first_at = lax.broadcasted_iota(jnp.int32, (16, GRID), 0).astype(F32)
    wide_at = [(first_at + float(k)).astype(BF16) for k in range(0, PARTS * GRID, 16)]
    low_at = wide_at[: LOW // 16]

    def put(j, carry):
        first = pl.multiple_of(j * lot, lot)
        values = [mixed[s, pl.ds(first, lot), :] for s in range(kept)]
        rows = rows_ref[pl.ds(first, lot), :]
        low = rows % LOW
        wide = (rows // LOW) * GRID + cols_ref[pl.ds(first, lot), :]
        lefts = []
        rights = []
        for g in range(lot):
            low_hit = hits(low_at, low[g : g + 1, :])
            lines = [jnp.broadcast_to(v[g : g + 1, :], (16, GRID)).astype(BF16) for v in values]
            lefts.append(jnp.concatenate([hit * line for line in lines for hit in low_hit], axis=0))
            rights.append(jnp.concatenate(hits(wide_at, wide[g : g + 1, :]), axis=0))
        grid[...] += lax.dot_general(
            jnp.concatenate(lefts, axis=1),
            jnp.concatenate(rights, axis=1),
            (((1,), (1,)), ((), ())),
            preferred_element_type=F32,
        )
        return carry

    lax.fori_loop(0, chunks // lot, put, 0)
    whole = jnp.concatenate(
        [
            grid[s * LOW : (s + 1) * LOW, p * GRID : (p + 1) * GRID]
            for s in range(kept)
            for p in range(PARTS)
        ],
        axis=0,
    ).astype(BF16)
    ahead = matmul(jnp.concatenate([whole, whole], axis=1), side_tall[...])
    backs = []
    for s in range(kept):
        high, rest = parted(ahead[s * GRID : (s + 1) * GRID])
        waves = matmul(basis_twice[...], jnp.concatenate([high, rest], axis=0)) + matmul(basis_low[...], high)
        high, rest = parted(waves * eigen_ref[...])
        both = matmul(side_both[...], high)
        backs.append(both[:GRID] + (both[GRID:] + matmul(side_both[:GRID, :], rest)))
    high, rest = parted(jnp.concatenate(backs, axis=0))
    both = matmul(high, basis_wide[...])
    smooth = both[:, :GRID] + (both[:, GRID:] + matmul(rest, basis_wide[:, :GRID]))
    for s in range(kept):
        for p in range(PARTS):
            top = s * GRID + p * LOW
            grid[s * LOW : (s + 1) * LOW, p * GRID : (p + 1) * GRID] = smooth[top : top + LOW]
    weighted = grid[...].astype(BF16)

    line_at = lax.broadcasted_iota(jnp.int32, (LOW, GRID), 0)

    def take(j, carry):
        first = pl.multiple_of(j * lot, lot)
        rows = rows_ref[pl.ds(first, lot), :]
        low = rows % LOW
        wide = (rows // LOW) * GRID + cols_ref[pl.ds(first, lot), :]
        rights = [jnp.concatenate(hits(wide_at, wide[g : g + 1, :]), axis=0) for g in range(lot)]
        picked = matmul(weighted, jnp.concatenate(rights, axis=1))
        hit = [line_at == low[g : g + 1, :] for g in range(lot)]
        for s in range(kept):
            lines = []
            for g in range(lot):
                block = picked[s * LOW : (s + 1) * LOW, g * GRID : (g + 1) * GRID]
                lines.append(jnp.sum(jnp.where(hit[g], block, 0.0), axis=0, keepdims=True))
            span = pl.ds(pl.multiple_of(s * chunks + first, lot), lot)
            out_ref[span, :] = jnp.concatenate(lines, axis=0).astype(BF16)
        return carry

    lax.fori_loop(0, chunks // lot, take, 0)


def spatial(which, weight, field, rows, cols, kept):
    chunks = field.shape[1]
    constants = [jnp.asarray(c) for c in spectrum()]
    return pl.pallas_call(
        functools.partial(spatial_kernel, 64, kept),
        out_shape=jax.ShapeDtypeStruct((kept * chunks, GRID), BF16),
        in_specs=[SMEM] + [VMEM] * (4 + len(constants)),
        out_specs=VMEM,
        scratch_shapes=[
            pltpu.VMEM((kept, chunks, GRID), F32),
            pltpu.VMEM((kept * LOW, PARTS * GRID), F32),
        ],
        compiler_params=pltpu.CompilerParams(vmem_limit_bytes=48 << 20),
        cost_estimate=pl.CostEstimate(flops=10**10, bytes_accessed=18 << 20, transcendentals=0),
    )(which, weight, field, rows, cols, *constants)


def opening_kernel(half_ref, duals_ref, coords_ref, out_ref):
    width = coords_ref.shape[1]
    picked = jnp.where(half_ref[0] == 0, coords_ref[0:1, :], coords_ref[1:2, :]).astype(F32)
    lines = [picked[:, k : k + GRID] for k in range(0, width, GRID)]
    block = jnp.concatenate([duals_ref[...].astype(F32), *lines], axis=0).astype(BF16)
    out_ref[...] = jnp.broadcast_to(block, out_ref.shape)


def opening(half, duals, coords, count):
    rows = duals.shape[0] + coords.shape[1] // GRID
    return pl.pallas_call(
        opening_kernel,
        out_shape=jax.ShapeDtypeStruct((count, rows, GRID), BF16),
        in_specs=[SMEM, VMEM, VMEM],
        out_specs=VMEM,
        compiler_params=pltpu.CompilerParams(vmem_limit_bytes=2 << 20),
    )(half, duals, coords)


def picking_kernel(here_ref, core_ref, owner_ref, time_ref, flat_ref, out_ref):
    count = owner_ref.shape[0]
    pair = 2
    lane = lax.broadcasted_iota(jnp.int32, (1, GRID), 1)
    ids = [jnp.where(time_ref[k : k + 1, :] >= here_ref[0], lane + k * GRID, -1) for k in range(count)]
    ids = jnp.concatenate(ids, axis=1).astype(F32)
    owners = owner_ref[...].astype(F32)
    first = core_ref[0] == 0
    order = []
    for side in range(pair):
        for k in range(0, count, pair):
            other, same = owners[k + 1 - side : k + 2 - side], owners[k + side : k + side + 1]
            order.append(jnp.where(first, other, same))
    slots = jnp.concatenate(order, axis=0).T
    flat = flat_ref[...]
    for k in range(count):
        chosen = jnp.where(slots[:, k : k + 1] == ids, 1.0, 0.0).astype(BF16)
        out_ref[k * GRID : (k + 1) * GRID, :] = matmul(chosen, flat).astype(BF16)


def picking(here, core, obs_owner, obs_time, flat):
    return pl.pallas_call(
        picking_kernel,
        out_shape=jax.ShapeDtypeStruct(flat.shape, BF16),
        in_specs=[SMEM] * 2 + [VMEM] * 3,
        out_specs=VMEM,
        compiler_params=pltpu.CompilerParams(vmem_limit_bytes=24 << 20),
        cost_estimate=pl.CostEstimate(flops=2 * flat.size * flat.shape[0], bytes_accessed=4 * flat.size, transcendentals=0),
    )(here, core, obs_owner.reshape(-1, GRID), obs_time.reshape(-1, GRID), flat)


def adjoint_kernel(here_ref, time_ref, duals_ref, flat_ref, out_ref, held, sent):
    pair, groups, rows, reals = duals_ref.shape
    outer, again, part, folds, _ = out_ref.shape
    keep = jnp.where(time_ref[...] >= here_ref[0], 1.0, 0.0).T
    seen = []
    for k in range(pair * groups):
        column = jnp.broadcast_to(keep[:, k : k + 1], (rows, reals)).astype(BF16)
        seen.append(duals_ref[k % pair, k // pair] * column)
    total = lax.dot_general(
        jnp.concatenate(seen, axis=0), flat_ref[...], (((0,), (0,)), ((), ())), preferred_element_type=F32
    )
    copies_out = []
    for i in range(outer):
        held[i] = total[i * part : (i + 1) * part].reshape(part, folds, GRID).astype(BF16)
        for j in range(again):
            copies_out.append(pltpu.make_async_copy(held.at[i], out_ref.at[i, j], sent.at[i, j]))
            copies_out[-1].start()
    for copy in copies_out:
        copy.wait()


def adjoint(here, obs_time, duals, flat, outer, again):
    rows, reals = duals.shape[2:]
    return pl.pallas_call(
        adjoint_kernel,
        out_shape=jax.ShapeDtypeStruct((outer, again, reals // outer, flat.shape[1] // GRID, GRID), BF16),
        in_specs=[SMEM] + [VMEM] * 3,
        out_specs=pl.BlockSpec(memory_space=pl.ANY),
        scratch_shapes=[
            pltpu.VMEM((outer, reals // outer, flat.shape[1] // GRID, GRID), BF16),
            pltpu.SemaphoreType.DMA((outer, again)),
        ],
        compiler_params=pltpu.CompilerParams(vmem_limit_bytes=24 << 20),
    )(here, obs_time.reshape(-1, rows), duals, flat)


def exchange(pieces, axes):
    return lax.all_to_all(pieces, axes, split_axis=0, concat_axis=0, tiled=True)


def copies(array, axes):
    return exchange(jnp.broadcast_to(array, (lax.axis_size(axes), *array.shape)), axes)


def per_device(sensitivity, duals, time_cov, cell_coords, obs_time, obs_owner):
    obs = sensitivity.shape[0]
    own, reals = duals.shape
    flat = sensitivity.reshape(obs, -1)
    here = lax.axis_index((X, ZH, CO)).reshape(1)
    core = lax.axis_index(CO).reshape(1)
    nx, nh, pair = (lax.axis_size(a) for a in (X, ZH, CO))
    which = lax.axis_index((ZH, CO)).reshape(1)

    plane = (ZH, Y, ZL)
    first = opening(lax.axis_index(ZH).reshape(1), duals, cell_coords, lax.axis_size(plane))
    even = core[0] == 0
    first, here, core, which, even = lax.optimization_barrier((first, here, core, which, even))
    first = exchange(first, plane)
    coords = first[:, own:].reshape(nh, -1, GRID).astype(jnp.int32)
    second = copies(first[:, :own].reshape(-1, reals), X)
    third = lax.all_gather(second.reshape(nx * nh, -1, reals), CO, axis=0)
    pieces = adjoint(here, obs_time, third, flat, nx, nh)
    pieces, owner = lax.optimization_barrier((pieces, obs_owner))
    field = exchange(pieces.reshape(-1, *pieces.shape[3:]), (X, ZH, Y, ZL))
    picked = picking(here, core, owner, obs_time, flat)
    field, picked = lax.optimization_barrier((field, picked))
    field = lax.all_gather(field.reshape(nx * nh, -1, GRID), CO, axis=0, tiled=True)

    weighted = spatial(which, time_cov, field, coords[0], coords[1], nx)
    weighted = exchange(weighted.reshape(reals, -1, GRID), (X, Y, ZL)).reshape(reals, -1)
    theirs, ours = (
        lax.dot_general(rows, weighted, (((1,), (1,)), ((), ())), preferred_element_type=F32)
        for rows in jnp.split(picked, pair)
    )
    swapped = lax.all_gather(theirs.astype(BF16), CO, axis=0)
    got = jnp.where(even, swapped[1], swapped[0])
    product = (ours + got.astype(F32)).astype(BF16)
    product = exchange(product.reshape(-1, own, reals), (X, ZH, Y, ZL))
    return jnp.sum(product.astype(F32), axis=0)


def solution(mesh):
    split = Mesh(mesh.devices.reshape(4, 2, 2, 8, 4), EVERY)
    every = P(EVERY, None)
    return jax.shard_map(
        per_device,
        mesh=split,
        in_specs=(P(None, (X, ZH, CO), CELL), every, P(), P(None, CELL), P(), P()),
        out_specs=every,
        check_vma=False,
    )
```
